32 devices in a mesh: az: 4 (over y, x), ta: 8 (over z, core).
Axes of the slice: x: 2, y: 2, z: 4, core: 2. Of those that a mesh axis runs over, the one named last changes fastest.
Arguments:
- initial_field: float32 [16, 1024, 4096], P(None, 'ta', 'az'), may hold values from -6 to 6
- conductivity: bfloat16 [16, 1024, 4096], P(None, 'ta', 'az'), may hold values from 0.25 to 4
- current_density: bfloat16 [16, 1024, 4096], P(None, 'ta', 'az'), may hold values from -6 to 6
- rotor_cycle: bfloat16 [1024, 4096], P('ta', 'az'), may hold values from -6 to 6
- skew_list: int32 [1024], P('ta'), may hold values from 0 to 31
Outputs:
- relaxed: float32 [16, 1024, 4096], P(None, 'ta', 'az')
The draws below stay inside these ranges and needn't reach their ends.
Inputs may be any that keep to these rules, and one draw needn't show every extreme that they name: `skew_list`: the rotor's offset in whole panels of 128 azimuth cells at each time step.
All inputs are finite; a program needn't handle non-finite values.
Results may differ from the reference program's by a relative error of at most 0.0003.
Values may be sent and summed in bfloat16 or wider, within the bound.
No kernel may reach another device: no remote copies, remote signals or barrier semaphores. Data moves between devices by JAX's collectives and lax.ppermute only.
A program may use at most 192 MiB of HBM per device.

```python
import math
import jax
import jax.numpy as jnp
from jax import lax

R = 16
SWEEPS = 2
NA = 4096
NT = 1024
NPANELS = 32


def touch_ends(entries, key, smallest, largest):
    extent = entries.shape
    place = [jax.random.randint(jax.random.fold_in(key, axis), (), 0, extent[axis]) for axis in range(len(extent))]
    entries = entries.at[tuple(place)].set(smallest)
    longest = extent.index(max(extent))
    place[longest] = (place[longest] + 1) % extent[longest]
    return entries.at[tuple(place)].set(largest)


def block_levels(key, dims, shards, low, top_value):
    def one(axis_at, blocks):
        heights = jax.random.uniform(jax.random.fold_in(jax.random.fold_in(key, 6), axis_at), (blocks,), jnp.float32, low / len(shards), top_value / len(shards))
        return jnp.repeat(jnp.exp(heights), dims[axis_at] // blocks).reshape((-1,) + (1,) * (len(dims) - axis_at - 1))

    gain = one(*shards[0])
    for cut in shards[1:]:
        gain = gain * one(*cut)
    return gain


def gaussian(stream_key, extent, spread, bound, split=(), kind=jnp.bfloat16):
    gain = block_levels(stream_key, extent, split, -0.22, 0.18) if split else 1.0
    entries = jax.random.normal(stream_key, extent, jnp.float32) * spread * gain
    return jnp.minimum(jnp.maximum(entries, -bound), bound).astype(kind)


def setup_inputs(seed: int = 0) -> dict:
    arg_keys = jax.random.split(jax.random.key(seed), 6)
    initial_field = gaussian(arg_keys[0], (R, NT, NA), 1.0, 6.0, ((1, 8), (2, 4)), jnp.float32)
    conductivity = jnp.clip(jnp.exp(math.log(4.0) - 2.7725887 * jax.random.uniform(arg_keys[1], (R, NT, NA), jnp.float32) ** block_levels(arg_keys[1], (R, NT, NA), ((1, 8), (2, 4)), -0.2, 0.2)), 0.25, 4.0).astype(jnp.bfloat16)
    current_density = gaussian(arg_keys[2], (R, NT, NA), 1.0, 6.0, ((1, 8), (2, 4)))
    rotor_cycle = gaussian(arg_keys[3], (NT, NA), 1.0, 6.0, ((0, 8), (1, 4)))
    skew_list = touch_ends(jax.random.randint(arg_keys[4], (NT,), 0, NPANELS), jax.random.fold_in(arg_keys[4], 1), 0, NPANELS - 1).astype(jnp.int32)
    return {"initial_field": initial_field, "conductivity": conductivity, "current_density": current_density, "rotor_cycle": rotor_cycle, "skew_list": skew_list}


COEF_RADIAL = 1.0
COEF_AZIM = 1.0
COEF_TIME = 1.0 / 12.0
DIAGONAL = 4.0


def half_step(field_now, cycle_map, conductivity, current_density, colour):
    zero_layer = jnp.zeros((1, NT, NA), jnp.float32)
    stacked = jnp.concatenate([cycle_map.astype(jnp.float32)[None], field_now, zero_layer], 0)
    time_ids = jnp.arange(NT, dtype=jnp.int32)
    azim_ids = jnp.arange(NA, dtype=jnp.int32)
    plane_parity = time_ids[:, None] + azim_ids[None, :]

    def relax_layer(layer_no):
        middle = stacked[layer_no + 1]
        radial = stacked[layer_no] + stacked[layer_no + 2]
        azimuthal = jnp.roll(middle, 1, 1) + jnp.roll(middle, -1, 1)
        temporal = (-jnp.roll(middle, -2, 0) + 8.0 * jnp.roll(middle, -1, 0)
                    - 8.0 * jnp.roll(middle, 1, 0) + jnp.roll(middle, 2, 0))
        sigma = conductivity[layer_no].astype(jnp.float32)
        source = current_density[layer_no].astype(jnp.float32)
        update = (source + COEF_RADIAL * radial + COEF_AZIM * azimuthal - COEF_TIME * sigma * temporal) / DIAGONAL
        parity = jnp.remainder(plane_parity + layer_no, 2)
        return jnp.where(parity == colour, update, middle)

    return lax.map(relax_layer, jnp.arange(R, dtype=jnp.int32))


def reference(initial_field, conductivity, current_density, rotor_cycle, skew_list):
    columns = jnp.remainder(jnp.arange(NA, dtype=jnp.int32)[None, :] - 128 * skew_list[:, None], NA).astype(jnp.int32)
    cycle_map = jnp.take_along_axis(rotor_cycle, columns, axis=1)
    field_now = initial_field
    for sweep_no in range(SWEEPS):
        field_now = half_step(field_now, cycle_map, conductivity, current_density, 0)
        field_now = half_step(field_now, cycle_map, conductivity, current_density, 1)
    return field_now
```

```python
import functools

import jax
import jax.numpy as jnp
from jax import lax
from jax.experimental import pallas as pl
from jax.experimental.pallas import tpu as pltpu
from jax.sharding import PartitionSpec as P

LANES = 128
EDGE = 8
LAG = 4
VMEM_BYTES = 60 * 1024 * 1024


def checker(rows):
    sub = lax.broadcasted_iota(jnp.int32, (rows, LANES), 0)
    lane = lax.broadcasted_iota(jnp.int32, (rows, LANES), 1)
    return ((sub + lane) & 1) == 0


def f32(value):
    return value.astype(jnp.float32)


def split_high_low(value):
    high = f32(value.astype(jnp.bfloat16))
    return high, value - high


def edges_kernel(
    u_top, u_bot, s_top, s_bot, j_top, j_bot,
    u_left, u_right, s_left, s_right, j_left, j_right,
    to_prev, to_next, to_left, to_right, *, pairs, tiles, blocks,
):
    even8 = checker(8)
    even16 = checker(16)
    sub = lax.broadcasted_iota(jnp.int32, (8, LANES), 0)
    lane = lax.broadcasted_iota(jnp.int32, (16, LANES), 1)
    field_rows = sub < 5

    def pair_rows(m, _):
        for c in range(tiles):
            cols = slice(c * LANES, (c + 1) * LANES)
            for u_ref, s_ref, j_ref, half, out_ref in (
                (u_top, s_top, j_top, 0, to_prev),
                (u_bot, s_bot, j_bot, 8, to_next),
            ):
                eo = []
                for ref in (u_ref, s_ref, j_ref):
                    first = f32(ref[2 * m, :, cols])
                    second = f32(ref[2 * m + 1, :, cols])
                    if first.shape[0] == 16:
                        first = first[half : half + 8]
                        second = second[half : half + 8]
                    eo.append((first, second))
                for colour in (0, 1):
                    pick = [
                        jnp.where(even8, a, b) if colour == 0 else jnp.where(even8, b, a)
                        for a, b in eo
                    ]
                    high, low = split_high_low(pick[0])
                    sig, cur = pick[1], pick[2]
                    if half == 0:
                        sig = pltpu.roll(sig, 5, 0)
                        cur = pltpu.roll(cur, 5, 0)
                    else:
                        high = pltpu.roll(high, 5, 0)
                        low = pltpu.roll(low, 5, 0)
                    both = jnp.concatenate(
                        [jnp.where(field_rows, high, sig), jnp.where(field_rows, low, cur)], 0
                    )
                    out_ref[colour, m, :, cols] = both.astype(jnp.bfloat16)
        return 0

    lax.fori_loop(0, pairs, pair_rows, 0)

    group_of = lane // 8
    first_half = (lane & 7) < 4

    def block_cols(q, _):
        rows = pl.ds(pl.multiple_of(16 * q, 16), 16)
        for refs, out_ref, red_first in (
            ((u_left, s_left, j_left), to_left, False),
            ((u_right, s_right, j_right), to_right, True),
        ):
            packed = []
            for ref in refs:
                acc = [jnp.zeros((8, LANES), jnp.float32)]
                total = acc[0]
                for m in range(pairs):
                    first = f32(ref[2 * m, rows, :])
                    second = f32(ref[2 * m + 1, rows, :])
                    red = jnp.where(even16, first, second)
                    black = jnp.where(even16, second, first)
                    for w in (0, 1):
                        g = m + pairs * w
                        near = pltpu.roll(red[8 * w : 8 * w + 8], (8 * g + 4) % LANES, 1)
                        far = pltpu.roll(black[8 * w : 8 * w + 8], (8 * g + 8) % LANES, 1)
                        if red_first:
                            near_slot, far_slot = 8 * g, 8 * g + 4
                        else:
                            near_slot, far_slot = 8 * g + 4, (8 * g + 8) % LANES
                        l8 = lane[:8]
                        total = jnp.where((l8 >= near_slot) & (l8 < near_slot + 4), near, total)
                        total = jnp.where((l8 >= far_slot) & (l8 < far_slot + 4), far, total)
                packed.append(total)
            high, low = split_high_low(packed[0])
            out_ref[q, 0] = jnp.concatenate([high, low], 0).astype(jnp.bfloat16)
            out_ref[q, 1] = jnp.concatenate([packed[1], packed[2]], 0).astype(jnp.bfloat16)
        return 0

    lax.fori_loop(0, blocks, block_cols, 0)


def pack_edges(field, sigma, current):
    layers, rows, cols = field.shape
    pairs, tiles, blocks = layers // 2, cols // LANES, rows // 16

    def whole(shape, index):
        return pl.BlockSpec(shape, lambda i: index)

    def row_specs(height):
        return [
            whole((layers, height, cols), (0, 0, 0)),
            whole((layers, height, cols), (0, rows // height - 1, 0)),
        ]

    col_specs = [
        whole((layers, rows, LANES), (0, 0, 0)),
        whole((layers, rows, LANES), (0, 0, tiles - 1)),
    ]
    ta_shape = (2, pairs, 16, cols)
    az_shape = (blocks, 2, 16, LANES)
    return pl.pallas_call(
        functools.partial(edges_kernel, pairs=pairs, tiles=tiles, blocks=blocks),
        grid=(1,),
        in_specs=row_specs(8) + row_specs(16) * 2 + col_specs * 3,
        out_specs=[whole(ta_shape, (0,) * 4)] * 2 + [whole(az_shape, (0,) * 4)] * 2,
        out_shape=[jax.ShapeDtypeStruct(ta_shape, jnp.bfloat16)] * 2
        + [jax.ShapeDtypeStruct(az_shape, jnp.bfloat16)] * 2,
        compiler_params=pltpu.CompilerParams(vmem_limit_bytes=VMEM_BYTES),
        name="edges",
    )(
        field, field, sigma, sigma, current, current,
        field, field, sigma, sigma, current, current,
    )


def relax_kernel(*refs, slots, pairs, rows, tiles):
    rotor = refs[:slots]
    (skew, from_left, from_right, corner_prev, corner_next, from_prev, from_next,
     u_ref, s_ref, j_ref, out_ref,
     red_a, red_b, black_a, black_b, sig_r, sig_b, cur_r, cur_b, side) = refs[slots:]
    g = pl.program_id(0)
    ext = rows + 2 * EDGE
    blocks = rows // 16
    even8 = checker(8)
    even16 = checker(16)
    lane = lax.broadcasted_iota(jnp.int32, (8, LANES), 1)
    lane16 = lax.broadcasted_iota(jnp.int32, (16, LANES), 1)
    lane_first = lane == 0
    lane_last = lane == LANES - 1

    @pl.when(g == 0)
    def prologue():
        panels = slots * tiles
        bits = (panels - 1).bit_length()
        want = [(panels - tiles - 1 + p) % panels for p in range(tiles + 2)]
        needs = [set(want)]
        for bit in range(bits):
            needs.append(needs[-1] | {(q - (1 << bit)) % panels for q in needs[-1]})

        def rotor_rows(b, _):
            at = pl.ds(pl.multiple_of(16 * b, 16), 16)
            turn = skew[at, :]
            cur = {}
            for q in sorted(needs[bits]):
                source = rotor[slots - 1 - q // tiles]
                c = q % tiles
                cur[q] = f32(source[at, c * LANES : (c + 1) * LANES])
            for bit in reversed(range(bits)):
                on = ((turn >> bit) & 1) == 1
                cur = {q: jnp.where(on, cur[(q - (1 << bit)) % panels], cur[q]) for q in sorted(needs[bit])}
            placed = [cur[want[p + 1]] for p in range(tiles)]
            placed.append(jnp.where(lane16 < LANES // 2, cur[want[tiles + 1]], cur[want[0]]))
            zero = jnp.zeros((16, LANES), jnp.float32)
            for buf in (red_a, red_b, black_a, black_b):
                for c in range(tiles + 1):
                    buf[0, c, at, :] = placed[c]
                    buf[pairs + 1, c, at, :] = zero
            return 0

        lax.fori_loop(0, ext // 16, rotor_rows, 0)

        left_slot = (lane & 7) < 4

        def decode(q, left, right):
            left0, left1, right0, right1 = f32(left[0]), f32(left[1]), f32(right[0]), f32(right[1])
            items = (
                (left0[:8] + left0[8:], right0[:8] + right0[8:], 1.0),
                (left1[:8], right1[:8], 1.0 / 48.0),
                (left1[8:], right1[8:], 0.25),
            )
            for item, (a, b, scale) in enumerate(items):
                side[0, item, q] = jnp.where(left_slot, a, b) * scale
                side[1, item, q] = jnp.where(left_slot, b, a) * scale

        for q in range(blocks):
            decode(q, from_left[q], from_right[q])
        decode(blocks, corner_prev[0], corner_prev[1])
        decode(blocks + 1, corner_next[0], corner_next[1])

    @pl.when(g < pairs)
    def load():
        m = g
        fields = ((red_a, sig_r, cur_r), (black_a, sig_b, cur_b))
        for colour in (0, 1):
            u_dst, s_dst, j_dst = fields[colour]
            for c in range(tiles):
                cols = slice(c * LANES, (c + 1) * LANES)
                both = f32(from_prev[colour, 0, :, cols])
                u_dst[m + 1, c, pl.ds(EDGE - 5, 8), :] = both[:8] + both[8:]
                s_dst[m, c, pl.ds(0, 8), :] = both[:8] * (1.0 / 48.0)
                j_dst[m, c, pl.ds(0, 8), :] = both[8:] * 0.25
                both = f32(from_next[colour, 0, :, cols])
                u_dst[m + 1, c, pl.ds(EDGE + rows, 8), :] = both[:8] + both[8:]
                s_dst[m, c, pl.ds(EDGE + rows - 5, 8), :] = both[:8] * (1.0 / 48.0)
                j_dst[m, c, pl.ds(EDGE + rows - 5, 8), :] = both[8:] * 0.25

        def own_rows(q, _):
            at = pl.ds(pl.multiple_of(16 * q, 16), 16)
            to = pl.ds(pl.multiple_of(16 * q + EDGE, 8), 16)
            for c in range(tiles):
                cols = slice(c * LANES, (c + 1) * LANES)
                a, b = u_ref[0, at, cols], u_ref[1, at, cols]
                red_a[m + 1, c, to, :] = jnp.where(even16, a, b)
                black_a[m + 1, c, to, :] = jnp.where(even16, b, a)
                a, b = f32(s_ref[0, at, cols]) * (1.0 / 48.0), f32(s_ref[1, at, cols]) * (1.0 / 48.0)
                sig_r[m, c, to, :] = jnp.where(even16, a, b)
                sig_b[m, c, to, :] = jnp.where(even16, b, a)
                a, b = f32(j_ref[0, at, cols]) * 0.25, f32(j_ref[1, at, cols]) * 0.25
                cur_r[m, c, to, :] = jnp.where(even16, a, b)
                cur_b[m, c, to, :] = jnp.where(even16, b, a)
            return 0

        lax.fori_loop(0, blocks, own_rows, 0)

        for colour in (0, 1):
            u_dst, s_dst, j_dst = fields[colour]
            for item, (dst, plane) in enumerate(((u_dst, m + 1), (s_dst, m), (j_dst, m))):
                for w in (0, 1):
                    turn = lax.rem(2 * LANES + 124 - 4 * colour - 8 * (m + pairs * w), LANES)
                    for q in range(blocks):
                        dst[plane, tiles, pl.ds(EDGE + 16 * q + 8 * w, 8), :] = pltpu.roll(side[colour, item, q], turn, 1)
                    if w == 1:
                        dst[plane, tiles, pl.ds(0, 8), :] = pltpu.roll(side[colour, item, blocks], turn, 1)
                    else:
                        dst[plane, tiles, pl.ds(EDGE + rows, 8), :] = pltpu.roll(side[colour, item, blocks + 1], turn, 1)

    def half_step(m, colour, own, other, sig, cur, start, count, write):
        def body(r, _):
            at = start + 8 * r
            centre = [other[m + 1, c, pl.ds(at, 8), :] for c in range(tiles + 1)]
            ahead = [pltpu.roll(x, 1, 1) for x in centre]
            back = [pltpu.roll(x, LANES - 1, 1) for x in centre]
            outputs = tiles if write is not None and count * 8 == rows else tiles + 1
            for c in range(outputs):
                left = jnp.where(lane_first, ahead[c - 1], ahead[c])
                right = jnp.where(lane_last, back[(c + 1) % (tiles + 1)], back[c])
                below = other[m, c, pl.ds(at, 8), :]
                above = other[m + 2, c, pl.ds(at, 8), :]
                outer = jnp.where(even8, below, above) if colour == 0 else jnp.where(even8, above, below)
                near = other[m + 1, c, pl.ds(at + 1, 8), :] - other[m + 1, c, pl.ds(at - 1, 8), :]
                far = own[m + 1, c, pl.ds(at + 2, 8), :] - own[m + 1, c, pl.ds(at - 2, 8), :]
                total = (left + right) + (centre[c] + outer)
                new = cur[m, c, pl.ds(at, 8), :] + 0.25 * total - sig[m, c, pl.ds(at, 8), :] * (8.0 * near - far)
                write(m, c, at, r, new)
            return 0

        lax.fori_loop(0, count, body, 0)

    def keep(buf):
        def write(m, c, at, r, new):
            buf[m + 1, c, pl.ds(at, 8), :] = new

        return write

    def emit(m, c, at, r, new):
        red = red_a[m + 1, c, pl.ds(at, 8), :]
        cols = slice(c * LANES, (c + 1) * LANES)
        to = pl.ds(pl.multiple_of(8 * r, 8), 8)
        out_ref[0, to, cols] = jnp.where(even8, red, new)
        out_ref[1, to, cols] = jnp.where(even8, new, red)

    wide = (EDGE - 4, rows // 8 + 1)
    plan = (
        (1, 0, red_a, black_a, sig_r, cur_r, wide, keep(red_b)),
        (2, 1, black_a, red_b, sig_b, cur_b, wide, keep(black_b)),
        (3, 0, red_b, black_b, sig_r, cur_r, wide, keep(red_a)),
        (4, 1, black_b, red_a, sig_b, cur_b, (EDGE, rows // 8), emit),
    )
    for lag, colour, own, other, sig, cur, (start, count), write in plan:

        @pl.when((g >= lag) & (g < pairs + lag))
        def phase(lag=lag, colour=colour, own=own, other=other, sig=sig, cur=cur, start=start, count=count, write=write):
            half_step(g - lag, colour, own, other, sig, cur, start, count, write)


def relax(rotor, skew, from_left, from_right, corner_prev, corner_next, from_prev, from_next, field, sigma, current):
    layers, rows, cols = field.shape
    pairs, tiles, slots = layers // 2, cols // LANES, len(rotor)
    ext = rows + 2 * EDGE

    def whole(array):
        zeros = (0,) * array.ndim
        return pl.BlockSpec(array.shape, lambda g: zeros)

    def coming(g):
        return jnp.minimum(g, pairs - 1)

    halo = pl.BlockSpec((2, 1, 16, cols), lambda g: (0, coming(g), 0, 0))
    block = pl.BlockSpec((2, rows, cols), lambda g: (coming(g), 0, 0))
    fixed = list(rotor) + [skew, from_left, from_right, corner_prev, corner_next]
    state = pltpu.VMEM((pairs + 2, tiles + 1, ext, LANES), jnp.float32)
    coef = pltpu.VMEM((pairs, tiles + 1, ext, LANES), jnp.float32)
    return pl.pallas_call(
        functools.partial(relax_kernel, slots=slots, pairs=pairs, rows=rows, tiles=tiles),
        grid=(pairs + LAG,),
        in_specs=[whole(a) for a in fixed] + [halo, halo, block, block, block],
        out_specs=pl.BlockSpec((2, rows, cols), lambda g: (jnp.maximum(g - LAG, 0), 0, 0)),
        out_shape=jax.ShapeDtypeStruct(field.shape, jnp.float32),
        scratch_shapes=[state] * 4 + [coef] * 4 + [pltpu.VMEM((2, 3, rows // 16 + 2, 8, LANES), jnp.float32)],
        compiler_params=pltpu.CompilerParams(vmem_limit_bytes=VMEM_BYTES),
        name="relax",
    )(*fixed, from_prev, from_next, field, sigma, current)


def moved(value, axis, steps):
    count = lax.axis_size(axis)
    return lax.ppermute(value, axis, [(i, (i + steps) % count) for i in range(count)])


def local(field, sigma, current, rotor_cycle, skew_list):
    rows = field.shape[1]
    rotor = jnp.concatenate(
        [moved(rotor_cycle[rows - EDGE :], "ta", 1), rotor_cycle, moved(rotor_cycle[:EDGE], "ta", -1)], 0
    )
    skew = jnp.concatenate(
        [moved(skew_list[rows - EDGE :], "ta", 1), skew_list, moved(skew_list[:EDGE], "ta", -1)], 0
    )
    skew = jnp.broadcast_to(skew[:, None], (rows + 2 * EDGE, LANES))
    to_prev, to_next, to_left, to_right = pack_edges(field, sigma, current)
    from_left = moved(to_right, "az", 1)
    from_right = moved(to_left, "az", -1)
    from_prev = moved(to_next, "ta", 1)
    from_next = moved(to_prev, "ta", -1)
    corner_prev = moved(jnp.stack([from_left[-1], from_right[-1]]), "ta", 1)
    corner_next = moved(jnp.stack([from_left[0], from_right[0]]), "ta", -1)
    slots = [rotor] + [moved(rotor, "az", s) for s in range(1, lax.axis_size("az"))]
    return relax(
        slots, skew, from_left, from_right, corner_prev, corner_next, from_prev, from_next, field, sigma, current
    )


def solution(mesh):
    placed = (P(None, "ta", "az"), P(None, "ta", "az"), P(None, "ta", "az"), P("ta", "az"), P("ta"))
    return jax.shard_map(
        local, mesh=mesh, in_specs=placed, out_specs=P(None, "ta", "az"), check_vma=False
    )
```

```python
import functools

import jax
import jax.numpy as jnp
from jax import lax
from jax.experimental import pallas as pl
from jax.experimental.pallas import tpu as pltpu
from jax.sharding import PartitionSpec as P

LANES = 128
EDGE = 8
LAG = 4
UNROLL = 6
SPANS = 3
VMEM_BYTES = 60 * 1024 * 1024


def checker(rows):
    sub = lax.broadcasted_iota(jnp.int32, (rows, LANES), 0)
    lane = lax.broadcasted_iota(jnp.int32, (rows, LANES), 1)
    return ((sub + lane) & 1) == 0


def f32(value):
    return value.astype(jnp.float32)


def split_high_low(value):
    high = f32(value.astype(jnp.bfloat16))
    return high, value - high


def edges_kernel(
    u_top, u_bot, s_top, s_bot, j_top, j_bot,
    u_left, u_right, s_left, s_right, j_left, j_right,
    to_prev, to_next, to_left, to_right, *, pairs, tiles, blocks,
):
    even8 = checker(8)
    even16 = checker(16)
    sub = lax.broadcasted_iota(jnp.int32, (8, LANES), 0)
    lane = lax.broadcasted_iota(jnp.int32, (16, LANES), 1)
    field_rows = sub < 5

    def pair_rows(m, _):
        for c in range(tiles):
            cols = slice(c * LANES, (c + 1) * LANES)
            for u_ref, s_ref, j_ref, half, out_ref in (
                (u_top, s_top, j_top, 0, to_prev),
                (u_bot, s_bot, j_bot, 8, to_next),
            ):
                eo = []
                for ref in (u_ref, s_ref, j_ref):
                    first = f32(ref[2 * m, :, cols])
                    second = f32(ref[2 * m + 1, :, cols])
                    if first.shape[0] == 16:
                        first = first[half : half + 8]
                        second = second[half : half + 8]
                    eo.append((first, second))
                for colour in (0, 1):
                    pick = [
                        jnp.where(even8, a, b) if colour == 0 else jnp.where(even8, b, a)
                        for a, b in eo
                    ]
                    high, low = split_high_low(pick[0])
                    sig, cur = pick[1], pick[2]
                    if half == 0:
                        sig = pltpu.roll(sig, 5, 0)
                        cur = pltpu.roll(cur, 5, 0)
                    else:
                        high = pltpu.roll(high, 5, 0)
                        low = pltpu.roll(low, 5, 0)
                    both = jnp.concatenate(
                        [jnp.where(field_rows, high, sig), jnp.where(field_rows, low, cur)], 0
                    )
                    out_ref[colour, m, :, cols] = both.astype(jnp.bfloat16)
        return 0

    lax.fori_loop(0, pairs, pair_rows, 0)

    group_of = lane // 8
    first_half = (lane & 7) < 4

    def block_cols(q, _):
        rows = pl.ds(pl.multiple_of(16 * q, 16), 16)
        for refs, out_ref, red_first in (
            ((u_left, s_left, j_left), to_left, False),
            ((u_right, s_right, j_right), to_right, True),
        ):
            packed = []
            for ref in refs:
                acc = [jnp.zeros((8, LANES), jnp.float32)]
                total = acc[0]
                for m in range(pairs):
                    first = f32(ref[2 * m, rows, :])
                    second = f32(ref[2 * m + 1, rows, :])
                    red = jnp.where(even16, first, second)
                    black = jnp.where(even16, second, first)
                    for w in (0, 1):
                        g = m + pairs * w
                        near = pltpu.roll(red[8 * w : 8 * w + 8], (8 * g + 4) % LANES, 1)
                        far = pltpu.roll(black[8 * w : 8 * w + 8], (8 * g + 8) % LANES, 1)
                        if red_first:
                            near_slot, far_slot = 8 * g, 8 * g + 4
                        else:
                            near_slot, far_slot = 8 * g + 4, (8 * g + 8) % LANES
                        l8 = lane[:8]
                        total = jnp.where((l8 >= near_slot) & (l8 < near_slot + 4), near, total)
                        total = jnp.where((l8 >= far_slot) & (l8 < far_slot + 4), far, total)
                packed.append(total)
            high, low = split_high_low(packed[0])
            out_ref[q, 0] = jnp.concatenate([high, low], 0).astype(jnp.bfloat16)
            out_ref[q, 1] = jnp.concatenate([packed[1], packed[2]], 0).astype(jnp.bfloat16)
        return 0

    lax.fori_loop(0, blocks, block_cols, 0)


def pack_edges(field, sigma, current):
    layers, rows, cols = field.shape
    pairs, tiles, blocks = layers // 2, cols // LANES, rows // 16

    def whole(shape, index):
        return pl.BlockSpec(shape, lambda i: index)

    def row_specs(height):
        return [
            whole((layers, height, cols), (0, 0, 0)),
            whole((layers, height, cols), (0, rows // height - 1, 0)),
        ]

    col_specs = [
        whole((layers, rows, LANES), (0, 0, 0)),
        whole((layers, rows, LANES), (0, 0, tiles - 1)),
    ]
    ta_shape = (2, pairs, 16, cols)
    az_shape = (blocks, 2, 16, LANES)
    return pl.pallas_call(
        functools.partial(edges_kernel, pairs=pairs, tiles=tiles, blocks=blocks),
        grid=(1,),
        in_specs=row_specs(8) + row_specs(16) * 2 + col_specs * 3,
        out_specs=[whole(ta_shape, (0,) * 4)] * 2 + [whole(az_shape, (0,) * 4)] * 2,
        out_shape=[jax.ShapeDtypeStruct(ta_shape, jnp.bfloat16)] * 2
        + [jax.ShapeDtypeStruct(az_shape, jnp.bfloat16)] * 2,
        compiler_params=pltpu.CompilerParams(vmem_limit_bytes=VMEM_BYTES),
        name="edges",
    )(
        field, field, sigma, sigma, current, current,
        field, field, sigma, sigma, current, current,
    )


def relax_kernel(*refs, slots, pairs, rows, tiles):
    rotor, rotor_edge = refs[:slots], refs[slots : 2 * slots]
    (skew, skew_edge, from_left, from_right, corner_prev, corner_next, from_prev, from_next,
     u_ref, s_ref, j_ref, out_ref,
     red_a, red_b, black_a, black_b, sig_r, sig_b, cur_r, cur_b, side) = refs[2 * slots :]
    g = pl.program_id(0)
    blocks = rows // 16
    even8 = checker(8)
    even16 = checker(16)
    lane = lax.broadcasted_iota(jnp.int32, (8, LANES), 1)
    lane16 = lax.broadcasted_iota(jnp.int32, (16, LANES), 1)
    lane_first = lane == 0
    lane_last = lane == LANES - 1

    @pl.when(g == 0)
    def prologue():
        panels = slots * tiles
        bits = (panels - 1).bit_length()
        want = [(panels - tiles - 1 + p) % panels for p in range(tiles + 2)]
        needs = [set(want)]
        for bit in range(bits):
            needs.append(needs[-1] | {(q - (1 << bit)) % panels for q in needs[-1]})

        def place(sources, at, turn, spots):
            cur = {}
            for q in sorted(needs[bits]):
                c = q % tiles
                cur[q] = f32(sources[slots - 1 - q // tiles][at, c * LANES : (c + 1) * LANES])
            for bit in reversed(range(bits)):
                on = ((turn >> bit) & 1) == 1
                cur = {q: jnp.where(on, cur[(q - (1 << bit)) % panels], cur[q]) for q in sorted(needs[bit])}
            placed = [cur[want[p + 1]] for p in range(tiles)]
            placed.append(jnp.where(lane16 < LANES // 2, cur[want[tiles + 1]], cur[want[0]]))
            zero = jnp.zeros((8, LANES), jnp.float32)
            for buf in (red_a, red_b, black_a, black_b):
                for c in range(tiles + 1):
                    for half, to in enumerate(spots):
                        buf[0, c, to, :] = placed[c][8 * half : 8 * half + 8]
                        buf[pairs + 1, c, to, :] = zero

        def rotor_rows(b, _):
            at = pl.ds(pl.multiple_of(16 * b, 16), 16)
            spots = [pl.ds(pl.multiple_of(16 * b + EDGE + 8 * half, 8), 8) for half in (0, 1)]
            place(rotor, at, skew[at, :], spots)
            return 0

        lax.fori_loop(0, blocks, rotor_rows, 0)
        place(rotor_edge, slice(0, 16), skew_edge[...].astype(jnp.int32), [pl.ds(0, 8), pl.ds(EDGE + rows, 8)])

        left_slot = (lane & 7) < 4

        def decode(q, left, right):
            left0, left1, right0, right1 = f32(left[0]), f32(left[1]), f32(right[0]), f32(right[1])
            items = (
                (left0[:8] + left0[8:], right0[:8] + right0[8:], 1.0),
                (left1[:8], right1[:8], 1.0 / 48.0),
                (left1[8:], right1[8:], 0.25),
            )
            for item, (a, b, scale) in enumerate(items):
                side[0, item, q] = jnp.where(left_slot, a, b) * scale
                side[1, item, q] = jnp.where(left_slot, b, a) * scale

        for q in range(blocks):
            decode(q, from_left[q], from_right[q])
        decode(blocks, corner_prev[0], corner_prev[1])
        decode(blocks + 1, corner_next[0], corner_next[1])

    @pl.when(g < pairs)
    def load():
        m = g
        fields = ((red_a, sig_r, cur_r), (black_a, sig_b, cur_b))
        for colour in (0, 1):
            u_dst, s_dst, j_dst = fields[colour]
            for c in range(tiles):
                cols = slice(c * LANES, (c + 1) * LANES)
                both = f32(from_prev[colour, 0, :, cols])
                u_dst[m + 1, c, pl.ds(EDGE - 5, 8), :] = both[:8] + both[8:]
                s_dst[m, c, pl.ds(0, 8), :] = both[:8] * (1.0 / 48.0)
                j_dst[m, c, pl.ds(0, 8), :] = both[8:] * 0.25
                both = f32(from_next[colour, 0, :, cols])
                u_dst[m + 1, c, pl.ds(EDGE + rows, 8), :] = both[:8] + both[8:]
                s_dst[m, c, pl.ds(EDGE + rows - 5, 8), :] = both[:8] * (1.0 / 48.0)
                j_dst[m, c, pl.ds(EDGE + rows - 5, 8), :] = both[8:] * 0.25

        def own_rows(q, _):
            at = pl.ds(pl.multiple_of(16 * q, 16), 16)
            to = pl.ds(pl.multiple_of(16 * q + EDGE, 8), 16)
            for c in range(tiles):
                cols = slice(c * LANES, (c + 1) * LANES)
                a, b = u_ref[0, at, cols], u_ref[1, at, cols]
                red_a[m + 1, c, to, :] = jnp.where(even16, a, b)
                black_a[m + 1, c, to, :] = jnp.where(even16, b, a)
                a, b = f32(s_ref[0, at, cols]) * (1.0 / 48.0), f32(s_ref[1, at, cols]) * (1.0 / 48.0)
                sig_r[m, c, to, :] = jnp.where(even16, a, b)
                sig_b[m, c, to, :] = jnp.where(even16, b, a)
                a, b = f32(j_ref[0, at, cols]) * 0.25, f32(j_ref[1, at, cols]) * 0.25
                cur_r[m, c, to, :] = jnp.where(even16, a, b)
                cur_b[m, c, to, :] = jnp.where(even16, b, a)
            return 0

        lax.fori_loop(0, blocks, own_rows, 0)

        for colour in (0, 1):
            u_dst, s_dst, j_dst = fields[colour]
            for item, (dst, plane) in enumerate(((u_dst, m + 1), (s_dst, m), (j_dst, m))):
                for w in (0, 1):
                    turn = lax.rem(2 * LANES + 124 - 4 * colour - 8 * (m + pairs * w), LANES)
                    for q in range(blocks):
                        dst[plane, tiles, pl.ds(EDGE + 16 * q + 8 * w, 8), :] = pltpu.roll(side[colour, item, q], turn, 1)
                    if w == 1:
                        dst[plane, tiles, pl.ds(0, 8), :] = pltpu.roll(side[colour, item, blocks], turn, 1)
                    else:
                        dst[plane, tiles, pl.ds(EDGE + rows, 8), :] = pltpu.roll(side[colour, item, blocks + 1], turn, 1)

    def half_step(m, colour, own, other, sig, cur, start, stride, outputs, write):
        def row_tile(at):
            centre = [other[m + 1, c, pl.ds(at, 8), :] for c in range(tiles + 1)]
            ahead = [pltpu.roll(x, 1, 1) for x in centre]
            back = [pltpu.roll(x, LANES - 1, 1) for x in centre]
            for c in range(outputs):
                left = jnp.where(lane_first, ahead[c - 1], ahead[c])
                right = jnp.where(lane_last, back[(c + 1) % (tiles + 1)], back[c])
                below = other[m, c, pl.ds(at, 8), :]
                above = other[m + 2, c, pl.ds(at, 8), :]
                outer = jnp.where(even8, below, above) if colour == 0 else jnp.where(even8, above, below)
                near = other[m + 1, c, pl.ds(at + 1, 8), :] - other[m + 1, c, pl.ds(at - 1, 8), :]
                far = own[m + 1, c, pl.ds(at + 2, 8), :] - own[m + 1, c, pl.ds(at - 2, 8), :]
                total = (left + right) + (centre[c] + outer)
                new = cur[m, c, pl.ds(at, 8), :] + 0.25 * total - sig[m, c, pl.ds(at, 8), :] * (8.0 * near - far)
                write(m, c, at, new)

        def body(r, _):
            for k in range(UNROLL):
                row_tile(start + stride * r + 8 * k)
            return 0

        lax.fori_loop(0, SPANS, body, 0)

    def keep(buf):
        def write(m, c, at, new):
            buf[m + 1, c, pl.ds(at, 8), :] = new

        return write

    def emit(m, c, at, new):
        red = red_a[m + 1, c, pl.ds(at, 8), :]
        cols = slice(c * LANES, (c + 1) * LANES)
        to = pl.ds(pl.multiple_of(at - EDGE, 8), 8)
        out_ref[0, to, cols] = jnp.where(even8, red, new)
        out_ref[1, to, cols] = jnp.where(even8, new, red)

    window = 8 * UNROLL
    wide = (EDGE - 4, (rows + 8 - window) // (SPANS - 1), tiles + 1)
    last = (EDGE, (rows - window) // (SPANS - 1), tiles)
    plan = (
        (1, 0, red_a, black_a, sig_r, cur_r, wide, keep(red_b)),
        (2, 1, black_a, red_b, sig_b, cur_b, wide, keep(black_b)),
        (3, 0, red_b, black_b, sig_r, cur_r, wide, keep(red_a)),
        (4, 1, black_b, red_a, sig_b, cur_b, last, emit),
    )
    for lag, colour, own, other, sig, cur, where, write in plan:

        @pl.when((g >= lag) & (g < pairs + lag))
        def phase(lag=lag, colour=colour, own=own, other=other, sig=sig, cur=cur, where=where, write=write):
            half_step(g - lag, colour, own, other, sig, cur, *where, write)


def relax(rotor, rotor_edge, skew, skew_edge, from_left, from_right, corner_prev, corner_next, from_prev, from_next, field, sigma, current):
    layers, rows, cols = field.shape
    pairs, tiles, slots = layers // 2, cols // LANES, len(rotor)
    ext = rows + 2 * EDGE

    def whole(array):
        zeros = (0,) * array.ndim
        return pl.BlockSpec(array.shape, lambda g: zeros)

    def coming(g):
        return jnp.minimum(g, pairs - 1)

    halo = pl.BlockSpec((2, 1, 16, cols), lambda g: (0, coming(g), 0, 0))
    block = pl.BlockSpec((2, rows, cols), lambda g: (coming(g), 0, 0))
    fixed = list(rotor) + list(rotor_edge) + [skew, skew_edge, from_left, from_right, corner_prev, corner_next]
    state = pltpu.VMEM((pairs + 2, tiles + 1, ext, LANES), jnp.float32)
    coef = pltpu.VMEM((pairs, tiles + 1, ext, LANES), jnp.float32)
    return pl.pallas_call(
        functools.partial(relax_kernel, slots=slots, pairs=pairs, rows=rows, tiles=tiles),
        grid=(pairs + LAG,),
        in_specs=[whole(a) for a in fixed] + [halo, halo, block, block, block],
        out_specs=pl.BlockSpec((2, rows, cols), lambda g: (jnp.maximum(g - LAG, 0), 0, 0)),
        out_shape=jax.ShapeDtypeStruct(field.shape, jnp.float32),
        scratch_shapes=[state] * 4 + [coef] * 4 + [pltpu.VMEM((2, 3, rows // 16 + 2, 8, LANES), jnp.float32)],
        compiler_params=pltpu.CompilerParams(vmem_limit_bytes=VMEM_BYTES),
        name="relax",
    )(*fixed, from_prev, from_next, field, sigma, current)


def moved(value, axis, steps):
    count = lax.axis_size(axis)
    return lax.ppermute(value, axis, [(i, (i + steps) % count) for i in range(count)])


def local(field, sigma, current, rotor_cycle, skew_list):
    rows, cols = field.shape[1:]
    shifts = range(1, lax.axis_size("az"))
    skew = jnp.broadcast_to(skew_list[:, None], (rows, LANES))
    slab = [
        jnp.concatenate([rotor_cycle[part], skew[part].astype(jnp.bfloat16)], 1)
        for part in (slice(rows - EDGE, rows), slice(0, EDGE))
    ]
    slab = jnp.concatenate([moved(slab[0], "ta", 1), moved(slab[1], "ta", -1)], 0)
    rotor = [rotor_cycle] + [moved(rotor_cycle, "az", s) for s in shifts]
    rotor_edge, skew_edge = slab[:, :cols], slab[:, cols:]
    rotor_edge = [rotor_edge] + [moved(rotor_edge, "az", s) for s in shifts]
    to_prev, to_next, to_left, to_right = pack_edges(field, sigma, current)
    from_left = moved(to_right, "az", 1)
    from_right = moved(to_left, "az", -1)
    from_prev = moved(to_next, "ta", 1)
    from_next = moved(to_prev, "ta", -1)
    corner_prev = moved(jnp.stack([from_left[-1], from_right[-1]]), "ta", 1)
    corner_next = moved(jnp.stack([from_left[0], from_right[0]]), "ta", -1)
    return relax(
        rotor, rotor_edge, skew, skew_edge, from_left, from_right, corner_prev, corner_next, from_prev, from_next, field, sigma, current
    )


def solution(mesh):
    placed = (P(None, "ta", "az"), P(None, "ta", "az"), P(None, "ta", "az"), P("ta", "az"), P("ta"))
    return jax.shard_map(
        local, mesh=mesh, in_specs=placed, out_specs=P(None, "ta", "az"), check_vma=False
    )
```

```python
import functools

import jax
import jax.numpy as jnp
from jax import lax
from jax.experimental import pallas as pl
from jax.experimental.pallas import tpu as pltpu
from jax.sharding import PartitionSpec as P

LANES = 128
EDGE = 8
LAG = 4
UNROLL = 6
SPANS = 3
VMEM_BYTES = 60 * 1024 * 1024


def checker(rows):
    sub = lax.broadcasted_iota(jnp.int32, (rows, LANES), 0)
    lane = lax.broadcasted_iota(jnp.int32, (rows, LANES), 1)
    return ((sub + lane) & 1) == 0


def f32(value):
    return value.astype(jnp.float32)


def split_high_low(value):
    high = f32(value.astype(jnp.bfloat16))
    return high, value - high


def edges_kernel(
    u_top, u_bot, s_top, s_bot, j_top, j_bot,
    u_left, u_right, s_left, s_right, j_left, j_right,
    to_prev, to_next, to_left, to_right, *, pairs, tiles, blocks,
):
    even8 = checker(8)
    even16 = checker(16)
    sub = lax.broadcasted_iota(jnp.int32, (8, LANES), 0)
    lane = lax.broadcasted_iota(jnp.int32, (16, LANES), 1)
    field_rows = sub < 5

    def pair_rows(m, _):
        for c in range(tiles):
            cols = slice(c * LANES, (c + 1) * LANES)
            for u_ref, s_ref, j_ref, half, out_ref in (
                (u_top, s_top, j_top, 0, to_prev),
                (u_bot, s_bot, j_bot, 8, to_next),
            ):
                eo = []
                for ref in (u_ref, s_ref, j_ref):
                    first = f32(ref[2 * m, :, cols])
                    second = f32(ref[2 * m + 1, :, cols])
                    if first.shape[0] == 16:
                        first = first[half : half + 8]
                        second = second[half : half + 8]
                    eo.append((first, second))
                for colour in (0, 1):
                    pick = [
                        jnp.where(even8, a, b) if colour == 0 else jnp.where(even8, b, a)
                        for a, b in eo
                    ]
                    high, low = split_high_low(pick[0])
                    sig, cur = pick[1], pick[2]
                    if half == 0:
                        sig = pltpu.roll(sig, 5, 0)
                        cur = pltpu.roll(cur, 5, 0)
                    else:
                        high = pltpu.roll(high, 5, 0)
                        low = pltpu.roll(low, 5, 0)
                    both = jnp.concatenate(
                        [jnp.where(field_rows, high, sig), jnp.where(field_rows, low, cur)], 0
                    )
                    out_ref[colour, m, :, cols] = both.astype(jnp.bfloat16)
        return 0

    lax.fori_loop(0, pairs, pair_rows, 0)

    group_of = lane // 8
    first_half = (lane & 7) < 4

    def block_cols(q, _):
        rows = pl.ds(pl.multiple_of(16 * q, 16), 16)
        for refs, out_ref, red_first in (
            ((u_left, s_left, j_left), to_left, False),
            ((u_right, s_right, j_right), to_right, True),
        ):
            packed = []
            for ref in refs:
                acc = [jnp.zeros((8, LANES), jnp.float32)]
                total = acc[0]
                for m in range(pairs):
                    first = f32(ref[2 * m, rows, :])
                    second = f32(ref[2 * m + 1, rows, :])
                    red = jnp.where(even16, first, second)
                    black = jnp.where(even16, second, first)
                    for w in (0, 1):
                        g = m + pairs * w
                        near = pltpu.roll(red[8 * w : 8 * w + 8], (8 * g + 4) % LANES, 1)
                        far = pltpu.roll(black[8 * w : 8 * w + 8], (8 * g + 8) % LANES, 1)
                        if red_first:
                            near_slot, far_slot = 8 * g, 8 * g + 4
                        else:
                            near_slot, far_slot = 8 * g + 4, (8 * g + 8) % LANES
                        l8 = lane[:8]
                        total = jnp.where((l8 >= near_slot) & (l8 < near_slot + 4), near, total)
                        total = jnp.where((l8 >= far_slot) & (l8 < far_slot + 4), far, total)
                packed.append(total)
            high, low = split_high_low(packed[0])
            out_ref[q, 0] = jnp.concatenate([high, low], 0).astype(jnp.bfloat16)
            out_ref[q, 1] = jnp.concatenate([packed[1], packed[2]], 0).astype(jnp.bfloat16)
        return 0

    lax.fori_loop(0, blocks, block_cols, 0)


def pack_edges(field, sigma, current):
    layers, rows, cols = field.shape
    pairs, tiles, blocks = layers // 2, cols // LANES, rows // 16

    def whole(shape, index):
        return pl.BlockSpec(shape, lambda i: index)

    def row_specs(height):
        return [
            whole((layers, height, cols), (0, 0, 0)),
            whole((layers, height, cols), (0, rows // height - 1, 0)),
        ]

    col_specs = [
        whole((layers, rows, LANES), (0, 0, 0)),
        whole((layers, rows, LANES), (0, 0, tiles - 1)),
    ]
    ta_shape = (2, pairs, 16, cols)
    az_shape = (blocks, 2, 16, LANES)
    return pl.pallas_call(
        functools.partial(edges_kernel, pairs=pairs, tiles=tiles, blocks=blocks),
        grid=(1,),
        in_specs=row_specs(8) + row_specs(16) * 2 + col_specs * 3,
        out_specs=[whole(ta_shape, (0,) * 4)] * 2 + [whole(az_shape, (0,) * 4)] * 2,
        out_shape=[jax.ShapeDtypeStruct(ta_shape, jnp.bfloat16)] * 2
        + [jax.ShapeDtypeStruct(az_shape, jnp.bfloat16)] * 2,
        compiler_params=pltpu.CompilerParams(vmem_limit_bytes=VMEM_BYTES),
        name="edges",
    )(
        field, field, sigma, sigma, current, current,
        field, field, sigma, sigma, current, current,
    )


def relax_kernel(*refs, slots, pairs, rows, tiles):
    (rotor, rotor_edge, skew, skew_edge, from_left, from_right, corner_prev, corner_next, from_prev, from_next,
     u_ref, s_ref, j_ref, out_ref,
     red_a, red_b, black_a, black_b, sig_r, sig_b, cur_r, cur_b, side) = refs
    g = pl.program_id(0)
    blocks = rows // 16
    even8 = checker(8)
    even16 = checker(16)
    lane = lax.broadcasted_iota(jnp.int32, (8, LANES), 1)
    lane16 = lax.broadcasted_iota(jnp.int32, (16, LANES), 1)
    lane_first = lane == 0
    lane_last = lane == LANES - 1

    @pl.when(g == 0)
    def prologue():
        panels = slots * tiles
        bits = (panels - 1).bit_length()
        here = lax.axis_index("az")
        device = [lax.rem(here + slots - r, slots) for r in range(slots)]
        want = [(panels - tiles - 1 + p) % panels for p in range(tiles + 2)]
        needs = [set(want)]
        for bit in range(bits):
            needs.append(needs[-1] | {(q - (1 << bit)) % panels for q in needs[-1]})

        def place(sources, at, turn, spots):
            cur = {}
            for q in sorted(needs[bits]):
                c = q % tiles
                cur[q] = f32(sources[device[slots - 1 - q // tiles], at, c * LANES : (c + 1) * LANES])
            for bit in reversed(range(bits)):
                on = ((turn >> bit) & 1) == 1
                cur = {q: jnp.where(on, cur[(q - (1 << bit)) % panels], cur[q]) for q in sorted(needs[bit])}
            placed = [cur[want[p + 1]] for p in range(tiles)]
            placed.append(jnp.where(lane16 < LANES // 2, cur[want[tiles + 1]], cur[want[0]]))
            zero = jnp.zeros((8, LANES), jnp.float32)
            for buf in (red_a, red_b, black_a, black_b):
                for c in range(tiles + 1):
                    for half, to in enumerate(spots):
                        buf[0, c, to, :] = placed[c][8 * half : 8 * half + 8]
                        buf[pairs + 1, c, to, :] = zero

        def rotor_rows(b, _):
            at = pl.ds(pl.multiple_of(16 * b, 16), 16)
            spots = [pl.ds(pl.multiple_of(16 * b + EDGE + 8 * half, 8), 8) for half in (0, 1)]
            place(rotor, at, skew[at, :], spots)
            return 0

        lax.fori_loop(0, blocks, rotor_rows, 0)
        place(rotor_edge, slice(0, 16), skew_edge[...].astype(jnp.int32), [pl.ds(0, 8), pl.ds(EDGE + rows, 8)])

        left_slot = (lane & 7) < 4

        def decode(q, left, right):
            left0, left1, right0, right1 = f32(left[0]), f32(left[1]), f32(right[0]), f32(right[1])
            items = (
                (left0[:8] + left0[8:], right0[:8] + right0[8:], 1.0),
                (left1[:8], right1[:8], 1.0 / 48.0),
                (left1[8:], right1[8:], 0.25),
            )
            for item, (a, b, scale) in enumerate(items):
                side[0, item, q] = jnp.where(left_slot, a, b) * scale
                side[1, item, q] = jnp.where(left_slot, b, a) * scale

        for q in range(blocks):
            decode(q, from_left[q], from_right[q])
        decode(blocks, corner_prev[0], corner_prev[1])
        decode(blocks + 1, corner_next[0], corner_next[1])

    @pl.when(g < pairs)
    def load():
        m = g
        fields = ((red_a, sig_r, cur_r), (black_a, sig_b, cur_b))
        for colour in (0, 1):
            u_dst, s_dst, j_dst = fields[colour]
            for c in range(tiles):
                cols = slice(c * LANES, (c + 1) * LANES)
                both = f32(from_prev[colour, 0, :, cols])
                u_dst[m + 1, c, pl.ds(EDGE - 5, 8), :] = both[:8] + both[8:]
                s_dst[m, c, pl.ds(0, 8), :] = both[:8] * (1.0 / 48.0)
                j_dst[m, c, pl.ds(0, 8), :] = both[8:] * 0.25
                both = f32(from_next[colour, 0, :, cols])
                u_dst[m + 1, c, pl.ds(EDGE + rows, 8), :] = both[:8] + both[8:]
                s_dst[m, c, pl.ds(EDGE + rows - 5, 8), :] = both[:8] * (1.0 / 48.0)
                j_dst[m, c, pl.ds(EDGE + rows - 5, 8), :] = both[8:] * 0.25

        def own_rows(q, _):
            at = pl.ds(pl.multiple_of(16 * q, 16), 16)
            to = pl.ds(pl.multiple_of(16 * q + EDGE, 8), 16)
            for c in range(tiles):
                cols = slice(c * LANES, (c + 1) * LANES)
                a, b = u_ref[0, at, cols], u_ref[1, at, cols]
                red_a[m + 1, c, to, :] = jnp.where(even16, a, b)
                black_a[m + 1, c, to, :] = jnp.where(even16, b, a)
                a, b = f32(s_ref[0, at, cols]) * (1.0 / 48.0), f32(s_ref[1, at, cols]) * (1.0 / 48.0)
                sig_r[m, c, to, :] = jnp.where(even16, a, b)
                sig_b[m, c, to, :] = jnp.where(even16, b, a)
                a, b = f32(j_ref[0, at, cols]) * 0.25, f32(j_ref[1, at, cols]) * 0.25
                cur_r[m, c, to, :] = jnp.where(even16, a, b)
                cur_b[m, c, to, :] = jnp.where(even16, b, a)
            return 0

        lax.fori_loop(0, blocks, own_rows, 0)

        for colour in (0, 1):
            u_dst, s_dst, j_dst = fields[colour]
            for item, (dst, plane) in enumerate(((u_dst, m + 1), (s_dst, m), (j_dst, m))):
                for w in (0, 1):
                    turn = lax.rem(2 * LANES + 124 - 4 * colour - 8 * (m + pairs * w), LANES)
                    for q in range(blocks):
                        dst[plane, tiles, pl.ds(EDGE + 16 * q + 8 * w, 8), :] = pltpu.roll(side[colour, item, q], turn, 1)
                    if w == 1:
                        dst[plane, tiles, pl.ds(0, 8), :] = pltpu.roll(side[colour, item, blocks], turn, 1)
                    else:
                        dst[plane, tiles, pl.ds(EDGE + rows, 8), :] = pltpu.roll(side[colour, item, blocks + 1], turn, 1)

    def half_step(m, colour, own, other, sig, cur, start, stride, outputs, write):
        def row_tile(at):
            centre = [other[m + 1, c, pl.ds(at, 8), :] for c in range(tiles + 1)]
            ahead = [pltpu.roll(x, 1, 1) for x in centre]
            back = [pltpu.roll(x, LANES - 1, 1) for x in centre]
            for c in range(outputs):
                left = jnp.where(lane_first, ahead[c - 1], ahead[c])
                right = jnp.where(lane_last, back[(c + 1) % (tiles + 1)], back[c])
                below = other[m, c, pl.ds(at, 8), :]
                above = other[m + 2, c, pl.ds(at, 8), :]
                outer = jnp.where(even8, below, above) if colour == 0 else jnp.where(even8, above, below)
                near = other[m + 1, c, pl.ds(at + 1, 8), :] - other[m + 1, c, pl.ds(at - 1, 8), :]
                far = own[m + 1, c, pl.ds(at + 2, 8), :] - own[m + 1, c, pl.ds(at - 2, 8), :]
                total = (left + right) + (centre[c] + outer)
                new = cur[m, c, pl.ds(at, 8), :] + 0.25 * total - sig[m, c, pl.ds(at, 8), :] * (8.0 * near - far)
                write(m, c, at, new)

        def body(r, _):
            for k in range(UNROLL):
                row_tile(start + stride * r + 8 * k)
            return 0

        lax.fori_loop(0, SPANS, body, 0)

    def keep(buf):
        def write(m, c, at, new):
            buf[m + 1, c, pl.ds(at, 8), :] = new

        return write

    def emit(m, c, at, new):
        red = red_a[m + 1, c, pl.ds(at, 8), :]
        cols = slice(c * LANES, (c + 1) * LANES)
        to = pl.ds(pl.multiple_of(at - EDGE, 8), 8)
        out_ref[0, to, cols] = jnp.where(even8, red, new)
        out_ref[1, to, cols] = jnp.where(even8, new, red)

    window = 8 * UNROLL
    wide = (EDGE - 4, (rows + 8 - window) // (SPANS - 1), tiles + 1)
    last = (EDGE, (rows - window) // (SPANS - 1), tiles)
    plan = (
        (1, 0, red_a, black_a, sig_r, cur_r, wide, keep(red_b)),
        (2, 1, black_a, red_b, sig_b, cur_b, wide, keep(black_b)),
        (3, 0, red_b, black_b, sig_r, cur_r, wide, keep(red_a)),
        (4, 1, black_b, red_a, sig_b, cur_b, last, emit),
    )
    for lag, colour, own, other, sig, cur, where, write in plan:

        @pl.when((g >= lag) & (g < pairs + lag))
        def phase(lag=lag, colour=colour, own=own, other=other, sig=sig, cur=cur, where=where, write=write):
            half_step(g - lag, colour, own, other, sig, cur, *where, write)


def relax(rotor, rotor_edge, skew, skew_edge, from_left, from_right, corner_prev, corner_next, from_prev, from_next, field, sigma, current):
    layers, rows, cols = field.shape
    pairs, tiles, slots = layers // 2, cols // LANES, rotor.shape[0]
    ext = rows + 2 * EDGE

    def whole(array):
        zeros = (0,) * array.ndim
        return pl.BlockSpec(array.shape, lambda g: zeros)

    def coming(g):
        return jnp.minimum(g, pairs - 1)

    halo = pl.BlockSpec((2, 1, 16, cols), lambda g: (0, coming(g), 0, 0))
    block = pl.BlockSpec((2, rows, cols), lambda g: (coming(g), 0, 0))
    fixed = [rotor, rotor_edge, skew, skew_edge, from_left, from_right, corner_prev, corner_next]
    state = pltpu.VMEM((pairs + 2, tiles + 1, ext, LANES), jnp.float32)
    coef = pltpu.VMEM((pairs, tiles + 1, ext, LANES), jnp.float32)
    return pl.pallas_call(
        functools.partial(relax_kernel, slots=slots, pairs=pairs, rows=rows, tiles=tiles),
        grid=(pairs + LAG,),
        in_specs=[whole(a) for a in fixed] + [halo, halo, block, block, block],
        out_specs=pl.BlockSpec((2, rows, cols), lambda g: (jnp.maximum(g - LAG, 0), 0, 0)),
        out_shape=jax.ShapeDtypeStruct(field.shape, jnp.float32),
        scratch_shapes=[state] * 4 + [coef] * 4 + [pltpu.VMEM((2, 3, rows // 16 + 2, 8, LANES), jnp.float32)],
        compiler_params=pltpu.CompilerParams(vmem_limit_bytes=VMEM_BYTES),
        name="relax",
    )(*fixed, from_prev, from_next, field, sigma, current)


def moved(value, axis, steps):
    count = lax.axis_size(axis)
    return lax.ppermute(value, axis, [(i, (i + steps) % count) for i in range(count)])


def local(field, sigma, current, rotor_cycle, skew_list):
    rows, cols = field.shape[1:]
    skew = jnp.broadcast_to(skew_list[:, None], (rows, LANES))
    slab = [
        jnp.concatenate([rotor_cycle[part], skew[part].astype(jnp.bfloat16)], 1)
        for part in (slice(rows - EDGE, rows), slice(0, EDGE))
    ]
    slab = jnp.concatenate([moved(slab[0], "ta", 1), moved(slab[1], "ta", -1)], 0)
    rotor = lax.all_gather(rotor_cycle, "az")
    rotor_edge = lax.all_gather(slab[:, :cols], "az")
    skew_edge = slab[:, cols:]
    to_prev, to_next, to_left, to_right = pack_edges(field, sigma, current)
    from_left = moved(to_right, "az", 1)
    from_right = moved(to_left, "az", -1)
    from_prev = moved(to_next, "ta", 1)
    from_next = moved(to_prev, "ta", -1)
    corner_prev = moved(jnp.stack([from_left[-1], from_right[-1]]), "ta", 1)
    corner_next = moved(jnp.stack([from_left[0], from_right[0]]), "ta", -1)
    return relax(
        rotor, rotor_edge, skew, skew_edge, from_left, from_right, corner_prev, corner_next, from_prev, from_next, field, sigma, current
    )


def solution(mesh):
    placed = (P(None, "ta", "az"), P(None, "ta", "az"), P(None, "ta", "az"), P("ta", "az"), P("ta"))
    return jax.shard_map(
        local, mesh=mesh, in_specs=placed, out_specs=P(None, "ta", "az"), check_vma=False
    )
```

```python
import functools

import jax
import jax.numpy as jnp
from jax import lax
from jax.experimental import pallas as pl
from jax.experimental.pallas import tpu as pltpu
from jax.sharding import PartitionSpec as P

LANES = 128
EDGE = 8
LAG = 4
UNROLL = 6
SPANS = 3
VMEM_BYTES = 60 * 1024 * 1024


def checker(rows):
    sub = lax.broadcasted_iota(jnp.int32, (rows, LANES), 0)
    lane = lax.broadcasted_iota(jnp.int32, (rows, LANES), 1)
    return ((sub + lane) & 1) == 0


def f32(value):
    return value.astype(jnp.float32)


def split_high_low(value):
    high = f32(value.astype(jnp.bfloat16))
    return high, value - high


def rows_kernel(u_top, u_bot, s_top, s_bot, j_top, j_bot, to_prev, to_next, *, pairs, tiles):
    even8 = checker(8)
    sub = lax.broadcasted_iota(jnp.int32, (8, LANES), 0)
    field_rows = sub < 5

    def pair_rows(m, _):
        for c in range(tiles):
            cols = slice(c * LANES, (c + 1) * LANES)
            for u_ref, s_ref, j_ref, half, out_ref in (
                (u_top, s_top, j_top, 0, to_prev),
                (u_bot, s_bot, j_bot, 8, to_next),
            ):
                eo = []
                for ref in (u_ref, s_ref, j_ref):
                    first = f32(ref[2 * m, :, cols])
                    second = f32(ref[2 * m + 1, :, cols])
                    if first.shape[0] == 16:
                        first = first[half : half + 8]
                        second = second[half : half + 8]
                    eo.append((first, second))
                for colour in (0, 1):
                    pick = [
                        jnp.where(even8, a, b) if colour == 0 else jnp.where(even8, b, a)
                        for a, b in eo
                    ]
                    high, low = split_high_low(pick[0])
                    sig, cur = pick[1], pick[2]
                    if half == 0:
                        sig = pltpu.roll(sig, 5, 0)
                        cur = pltpu.roll(cur, 5, 0)
                    else:
                        high = pltpu.roll(high, 5, 0)
                        low = pltpu.roll(low, 5, 0)
                    both = jnp.concatenate(
                        [jnp.where(field_rows, high, sig), jnp.where(field_rows, low, cur)], 0
                    )
                    out_ref[colour, m, :, cols] = both.astype(jnp.bfloat16)
        return 0

    lax.fori_loop(0, pairs, pair_rows, 0)


def cols_kernel(
    u_left, u_right, s_left, s_right, j_left, j_right, r_top, r_bot, k_top, k_bot,
    to_left, to_right, small_prev, small_next, *, pairs, tiles, blocks,
):
    even16 = checker(16)
    lane = lax.broadcasted_iota(jnp.int32, (16, LANES), 1)

    def block_cols(q, _):
        rows = pl.ds(pl.multiple_of(16 * q, 16), 16)
        for refs, out_ref, red_first in (
            ((u_left, s_left, j_left), to_left, False),
            ((u_right, s_right, j_right), to_right, True),
        ):
            packed = []
            for ref in refs:
                acc = [jnp.zeros((8, LANES), jnp.float32)]
                total = acc[0]
                for m in range(pairs):
                    first = f32(ref[2 * m, rows, :])
                    second = f32(ref[2 * m + 1, rows, :])
                    red = jnp.where(even16, first, second)
                    black = jnp.where(even16, second, first)
                    for w in (0, 1):
                        g = m + pairs * w
                        near = pltpu.roll(red[8 * w : 8 * w + 8], (8 * g + 4) % LANES, 1)
                        far = pltpu.roll(black[8 * w : 8 * w + 8], (8 * g + 8) % LANES, 1)
                        if red_first:
                            near_slot, far_slot = 8 * g, 8 * g + 4
                        else:
                            near_slot, far_slot = 8 * g + 4, (8 * g + 8) % LANES
                        l8 = lane[:8]
                        total = jnp.where((l8 >= near_slot) & (l8 < near_slot + 4), near, total)
                        total = jnp.where((l8 >= far_slot) & (l8 < far_slot + 4), far, total)
                packed.append(total)
            high, low = split_high_low(packed[0])
            out_ref[2 * q] = jnp.concatenate([high, low], 0).astype(jnp.bfloat16)
            out_ref[2 * q + 1] = jnp.concatenate([packed[1], packed[2]], 0).astype(jnp.bfloat16)
        return 0

    lax.fori_loop(0, blocks, block_cols, 0)
    for out_ref, near, r_ref, k_ref in (
        (small_prev, 0, r_top, k_top),
        (small_next, 2 * blocks - 2, r_bot, k_bot),
    ):
        for i in (0, 1):
            out_ref[i] = to_left[near + i]
            out_ref[2 + i] = to_right[near + i]
        for c in range(tiles):
            out_ref[4 + c] = r_ref[:, c * LANES : (c + 1) * LANES]
        out_ref[4 + tiles] = f32(k_ref[...]).astype(jnp.bfloat16)


def whole_at(shape, index):
    return pl.BlockSpec(shape, lambda i: index)


def pack_rows(field, sigma, current):
    layers, rows, cols = field.shape
    pairs, tiles = layers // 2, cols // LANES

    def row_specs(height):
        shape = (layers, height, cols)
        return [whole_at(shape, (0, 0, 0)), whole_at(shape, (0, rows // height - 1, 0))]

    shape = (2, pairs, 16, cols)
    return pl.pallas_call(
        functools.partial(rows_kernel, pairs=pairs, tiles=tiles),
        grid=(1,),
        in_specs=row_specs(8) + row_specs(16) * 2,
        out_specs=[whole_at(shape, (0,) * 4)] * 2,
        out_shape=[jax.ShapeDtypeStruct(shape, jnp.bfloat16)] * 2,
        compiler_params=pltpu.CompilerParams(vmem_limit_bytes=VMEM_BYTES),
        cost_estimate=pl.CostEstimate(flops=0, bytes_accessed=12 << 20, transcendentals=0),
        name="pack_rows",
    )(field, field, sigma, sigma, current, current)


def pack_cols(field, sigma, current, rotor_cycle, skew):
    layers, rows, cols = field.shape
    pairs, tiles, blocks = layers // 2, cols // LANES, rows // 16
    shape = (layers, rows, LANES)
    cols_specs = [whole_at(shape, (0, 0, 0)), whole_at(shape, (0, 0, tiles - 1))]
    rotor_specs = [whole_at((16, cols), (i, 0)) for i in (0, blocks - 1)]
    skew_specs = [whole_at((16, LANES), (i, 0)) for i in (0, blocks - 1)]
    out = [(2 * blocks, 16, LANES)] * 2 + [(tiles + 5, 16, LANES)] * 2
    return pl.pallas_call(
        functools.partial(cols_kernel, pairs=pairs, tiles=tiles, blocks=blocks),
        grid=(1,),
        in_specs=cols_specs * 3 + rotor_specs + skew_specs,
        out_specs=[whole_at(x, (0,) * 3) for x in out],
        out_shape=[jax.ShapeDtypeStruct(x, jnp.bfloat16) for x in out],
        compiler_params=pltpu.CompilerParams(vmem_limit_bytes=VMEM_BYTES),
        cost_estimate=pl.CostEstimate(flops=0, bytes_accessed=16 << 20, transcendentals=0),
        name="pack_cols",
    )(field, field, sigma, sigma, current, current, rotor_cycle, rotor_cycle, skew, skew)


def relax_kernel(*refs, slots, pairs, rows, tiles):
    rotor, refs = refs[:slots], refs[slots:]
    others, refs = refs[: slots - 3], refs[slots - 3 :]
    (skew, small_prev, small_next, from_left, from_right, from_prev, from_next,
     u_ref, s_ref, j_ref, out_ref,
     red_a, red_b, black_a, black_b, sig_r, sig_b, cur_r, cur_b, side) = refs
    g = pl.program_id(0)
    blocks = rows // 16
    even8 = checker(8)
    even16 = checker(16)
    lane = lax.broadcasted_iota(jnp.int32, (8, LANES), 1)
    lane16 = lax.broadcasted_iota(jnp.int32, (16, LANES), 1)
    lane_first = lane == 0
    lane_last = lane == LANES - 1

    @pl.when(g == 0)
    def prologue():
        panels = slots * tiles
        bits = (panels - 1).bit_length()
        want = [(panels - tiles - 1 + p) % panels for p in range(tiles + 2)]
        needs = [set(want)]
        for bit in range(bits):
            needs.append(needs[-1] | {(q - (1 << bit)) % panels for q in needs[-1]})

        def place(panel, turn, spots):
            cur = {q: f32(panel(slots - 1 - q // tiles, q % tiles)) for q in sorted(needs[bits])}
            for bit in reversed(range(bits)):
                on = ((turn >> bit) & 1) == 1
                cur = {q: jnp.where(on, cur[(q - (1 << bit)) % panels], cur[q]) for q in sorted(needs[bit])}
            placed = [cur[want[p + 1]] for p in range(tiles)]
            placed.append(jnp.where(lane16 < LANES // 2, cur[want[tiles + 1]], cur[want[0]]))
            zero = jnp.zeros((8, LANES), jnp.float32)
            for buf in (red_a, red_b, black_a, black_b):
                for c in range(tiles + 1):
                    for half, to in spots:
                        buf[0, c, to, :] = placed[c][8 * half : 8 * half + 8]
                        buf[pairs + 1, c, to, :] = zero

        def rotor_rows(b, _):
            at = pl.ds(pl.multiple_of(16 * b, 16), 16)
            spots = [(half, pl.ds(pl.multiple_of(16 * b + EDGE + 8 * half, 8), 8)) for half in (0, 1)]
            place(lambda r, c: rotor[r][at, c * LANES : (c + 1) * LANES], skew[at, :], spots)
            return 0

        lax.fori_loop(0, blocks, rotor_rows, 0)
        base = 2 * blocks + 4
        for small, first, spot in (
            (small_prev, 0, (1, pl.ds(0, 8))),
            (small_next, tiles, (0, pl.ds(EDGE + rows, 8))),
        ):

            def edge_panel(r, c, small=small, first=first):
                if r == 0:
                    return small[4 + c]
                if r == 1:
                    return from_left[base + first + c]
                if r == slots - 1:
                    return from_right[base + first + c]
                return others[r - 2][first + c]

            place(edge_panel, f32(small[4 + tiles]).astype(jnp.int32), [spot])

        left_slot = (lane & 7) < 4

        def decode(q, left, right):
            left0, left1, right0, right1 = f32(left[0]), f32(left[1]), f32(right[0]), f32(right[1])
            items = (
                (left0[:8] + left0[8:], right0[:8] + right0[8:], 1.0),
                (left1[:8], right1[:8], 1.0 / 48.0),
                (left1[8:], right1[8:], 0.25),
            )
            for item, (a, b, scale) in enumerate(items):
                side[0, item, q] = jnp.where(left_slot, a, b) * scale
                side[1, item, q] = jnp.where(left_slot, b, a) * scale

        for q in range(blocks + 2):
            pick = slice(2 * q, 2 * q + 2)
            decode(q, from_left[pick], from_right[pick])

    @pl.when(g < pairs)
    def load():
        m = g
        fields = ((red_a, sig_r, cur_r), (black_a, sig_b, cur_b))
        for colour in (0, 1):
            u_dst, s_dst, j_dst = fields[colour]
            for c in range(tiles):
                cols = slice(c * LANES, (c + 1) * LANES)
                both = f32(from_prev[colour, 0, :, cols])
                u_dst[m + 1, c, pl.ds(EDGE - 5, 8), :] = both[:8] + both[8:]
                s_dst[m, c, pl.ds(0, 8), :] = both[:8] * (1.0 / 48.0)
                j_dst[m, c, pl.ds(0, 8), :] = both[8:] * 0.25
                both = f32(from_next[colour, 0, :, cols])
                u_dst[m + 1, c, pl.ds(EDGE + rows, 8), :] = both[:8] + both[8:]
                s_dst[m, c, pl.ds(EDGE + rows - 5, 8), :] = both[:8] * (1.0 / 48.0)
                j_dst[m, c, pl.ds(EDGE + rows - 5, 8), :] = both[8:] * 0.25

        def own_rows(q, _):
            at = pl.ds(pl.multiple_of(16 * q, 16), 16)
            to = pl.ds(pl.multiple_of(16 * q + EDGE, 8), 16)
            for c in range(tiles):
                cols = slice(c * LANES, (c + 1) * LANES)
                a, b = u_ref[0, at, cols], u_ref[1, at, cols]
                red_a[m + 1, c, to, :] = jnp.where(even16, a, b)
                black_a[m + 1, c, to, :] = jnp.where(even16, b, a)
                a, b = f32(s_ref[0, at, cols]) * (1.0 / 48.0), f32(s_ref[1, at, cols]) * (1.0 / 48.0)
                sig_r[m, c, to, :] = jnp.where(even16, a, b)
                sig_b[m, c, to, :] = jnp.where(even16, b, a)
                a, b = f32(j_ref[0, at, cols]) * 0.25, f32(j_ref[1, at, cols]) * 0.25
                cur_r[m, c, to, :] = jnp.where(even16, a, b)
                cur_b[m, c, to, :] = jnp.where(even16, b, a)
            return 0

        lax.fori_loop(0, blocks, own_rows, 0)

        for colour in (0, 1):
            u_dst, s_dst, j_dst = fields[colour]
            for item, (dst, plane) in enumerate(((u_dst, m + 1), (s_dst, m), (j_dst, m))):
                for w in (0, 1):
                    turn = lax.rem(2 * LANES + 124 - 4 * colour - 8 * (m + pairs * w), LANES)
                    for q in range(blocks):
                        dst[plane, tiles, pl.ds(EDGE + 16 * q + 8 * w, 8), :] = pltpu.roll(side[colour, item, q], turn, 1)
                    if w == 1:
                        dst[plane, tiles, pl.ds(0, 8), :] = pltpu.roll(side[colour, item, blocks], turn, 1)
                    else:
                        dst[plane, tiles, pl.ds(EDGE + rows, 8), :] = pltpu.roll(side[colour, item, blocks + 1], turn, 1)

    def half_step(m, colour, own, other, sig, cur, start, stride, outputs, write):
        def row_tile(at):
            centre = [other[m + 1, c, pl.ds(at, 8), :] for c in range(tiles + 1)]
            ahead = [pltpu.roll(x, 1, 1) for x in centre]
            back = [pltpu.roll(x, LANES - 1, 1) for x in centre]
            for c in range(outputs):
                left = jnp.where(lane_first, ahead[c - 1], ahead[c])
                right = jnp.where(lane_last, back[(c + 1) % (tiles + 1)], back[c])
                below = other[m, c, pl.ds(at, 8), :]
                above = other[m + 2, c, pl.ds(at, 8), :]
                outer = jnp.where(even8, below, above) if colour == 0 else jnp.where(even8, above, below)
                near = other[m + 1, c, pl.ds(at + 1, 8), :] - other[m + 1, c, pl.ds(at - 1, 8), :]
                far = own[m + 1, c, pl.ds(at + 2, 8), :] - own[m + 1, c, pl.ds(at - 2, 8), :]
                total = (left + right) + (centre[c] + outer)
                new = cur[m, c, pl.ds(at, 8), :] + 0.25 * total - sig[m, c, pl.ds(at, 8), :] * (8.0 * near - far)
                write(m, c, at, new)

        def body(r, _):
            for k in range(UNROLL):
                row_tile(start + stride * r + 8 * k)
            return 0

        lax.fori_loop(0, SPANS, body, 0)

    def keep(buf):
        def write(m, c, at, new):
            buf[m + 1, c, pl.ds(at, 8), :] = new

        return write

    def emit(m, c, at, new):
        red = red_a[m + 1, c, pl.ds(at, 8), :]
        cols = slice(c * LANES, (c + 1) * LANES)
        to = pl.ds(pl.multiple_of(at - EDGE, 8), 8)
        out_ref[0, to, cols] = jnp.where(even8, red, new)
        out_ref[1, to, cols] = jnp.where(even8, new, red)

    window = 8 * UNROLL
    wide = (EDGE - 4, (rows + 8 - window) // (SPANS - 1), tiles + 1)
    last = (EDGE, (rows - window) // (SPANS - 1), tiles)
    plan = (
        (1, 0, red_a, black_a, sig_r, cur_r, wide, keep(red_b)),
        (2, 1, black_a, red_b, sig_b, cur_b, wide, keep(black_b)),
        (3, 0, red_b, black_b, sig_r, cur_r, wide, keep(red_a)),
        (4, 1, black_b, red_a, sig_b, cur_b, last, emit),
    )
    for lag, colour, own, other, sig, cur, where, write in plan:

        @pl.when((g >= lag) & (g < pairs + lag))
        def phase(lag=lag, colour=colour, own=own, other=other, sig=sig, cur=cur, where=where, write=write):
            half_step(g - lag, colour, own, other, sig, cur, *where, write)


def relax(rotor, others, skew, small_prev, small_next, from_left, from_right, from_prev, from_next, field, sigma, current):
    layers, rows, cols = field.shape
    pairs, tiles, slots = layers // 2, cols // LANES, len(rotor)
    ext = rows + 2 * EDGE

    def whole(array):
        zeros = (0,) * array.ndim
        return pl.BlockSpec(array.shape, lambda g: zeros)

    def coming(g):
        return jnp.minimum(g, pairs - 1)

    halo = pl.BlockSpec((2, 1, 16, cols), lambda g: (0, coming(g), 0, 0))
    block = pl.BlockSpec((2, rows, cols), lambda g: (coming(g), 0, 0))
    fixed = list(rotor) + list(others) + [skew, small_prev, small_next, from_left, from_right]
    state = pltpu.VMEM((pairs + 2, tiles + 1, ext, LANES), jnp.float32)
    coef = pltpu.VMEM((pairs, tiles + 1, ext, LANES), jnp.float32)
    return pl.pallas_call(
        functools.partial(relax_kernel, slots=slots, pairs=pairs, rows=rows, tiles=tiles),
        grid=(pairs + LAG,),
        in_specs=[whole(a) for a in fixed] + [halo, halo, block, block, block],
        out_specs=pl.BlockSpec((2, rows, cols), lambda g: (jnp.maximum(g - LAG, 0), 0, 0)),
        out_shape=jax.ShapeDtypeStruct(field.shape, jnp.float32),
        scratch_shapes=[state] * 4 + [coef] * 4 + [pltpu.VMEM((2, 3, rows // 16 + 2, 8, LANES), jnp.float32)],
        compiler_params=pltpu.CompilerParams(vmem_limit_bytes=VMEM_BYTES),
        name="relax",
    )(*fixed, from_prev, from_next, field, sigma, current)


def moved(value, axis, steps):
    count = lax.axis_size(axis)
    return lax.ppermute(value, axis, [(i, (i + steps) % count) for i in range(count)])


def local(field, sigma, current, rotor_cycle, skew_list):
    rows, cols = field.shape[1:]
    tiles = cols // LANES
    count = lax.axis_size("az")
    skew = jnp.broadcast_to(skew_list[:, None], (rows, LANES))
    rotor = [rotor_cycle] + [moved(rotor_cycle, "az", s) for s in range(1, count)]
    to_prev, to_next = pack_rows(field, sigma, current)
    from_prev = moved(to_next, "ta", 1)
    from_next = moved(to_prev, "ta", -1)
    to_left, to_right, small_to_prev, small_to_next = pack_cols(field, sigma, current, rotor_cycle, skew)
    small_prev = moved(small_to_next, "ta", 1)
    small_next = moved(small_to_prev, "ta", -1)
    rotor_edge = [small_prev[4 : 4 + tiles], small_next[4 : 4 + tiles]]
    from_right = moved(jnp.concatenate([to_left, small_prev[:2], small_next[:2]] + rotor_edge), "az", -1)
    from_left = moved(jnp.concatenate([to_right, small_prev[2:4], small_next[2:4]] + rotor_edge), "az", 1)
    rotor_edge = jnp.concatenate(rotor_edge)
    others = [moved(rotor_edge, "az", s) for s in range(2, count - 1)]
    return relax(
        rotor, others, skew, small_prev, small_next, from_left, from_right, from_prev, from_next,
        field, sigma, current,
    )


def solution(mesh):
    placed = (P(None, "ta", "az"), P(None, "ta", "az"), P(None, "ta", "az"), P("ta", "az"), P("ta"))
    return jax.shard_map(
        local, mesh=mesh, in_specs=placed, out_specs=P(None, "ta", "az"), check_vma=False
    )
```

```python
import functools

import jax
import jax.numpy as jnp
from jax import lax
from jax.experimental import pallas as pl
from jax.experimental.pallas import tpu as pltpu
from jax.sharding import PartitionSpec as P

LANES = 128
EDGE = 8
LAG = 4
UNROLL = 6
SPANS = 3
VMEM_BYTES = 60 * 1024 * 1024


def checker(rows):
    sub = lax.broadcasted_iota(jnp.int32, (rows, LANES), 0)
    lane = lax.broadcasted_iota(jnp.int32, (rows, LANES), 1)
    return ((sub + lane) & 1) == 0


def f32(value):
    return value.astype(jnp.float32)


def split_high_low(value):
    high = f32(value.astype(jnp.bfloat16))
    return high, value - high


def rows_kernel(u_top, u_bot, s_top, s_bot, j_top, j_bot, to_prev, to_next, *, pairs, tiles):
    even8 = checker(8)
    sub = lax.broadcasted_iota(jnp.int32, (8, LANES), 0)
    field_rows = sub < 5

    def pair_rows(m, _):
        for c in range(tiles):
            cols = slice(c * LANES, (c + 1) * LANES)
            for u_ref, s_ref, j_ref, half, out_ref in (
                (u_top, s_top, j_top, 0, to_prev),
                (u_bot, s_bot, j_bot, 8, to_next),
            ):
                eo = []
                for ref in (u_ref, s_ref, j_ref):
                    first = f32(ref[2 * m, :, cols])
                    second = f32(ref[2 * m + 1, :, cols])
                    if first.shape[0] == 16:
                        first = first[half : half + 8]
                        second = second[half : half + 8]
                    eo.append((first, second))
                for colour in (0, 1):
                    pick = [
                        jnp.where(even8, a, b) if colour == 0 else jnp.where(even8, b, a)
                        for a, b in eo
                    ]
                    high, low = split_high_low(pick[0])
                    sig, cur = pick[1], pick[2]
                    if half == 0:
                        sig = pltpu.roll(sig, 5, 0)
                        cur = pltpu.roll(cur, 5, 0)
                    else:
                        high = pltpu.roll(high, 5, 0)
                        low = pltpu.roll(low, 5, 0)
                    both = jnp.concatenate(
                        [jnp.where(field_rows, high, sig), jnp.where(field_rows, low, cur)], 0
                    )
                    out_ref[colour, m, :, cols] = both.astype(jnp.bfloat16)
        return 0

    lax.fori_loop(0, pairs, pair_rows, 0)


def cols_kernel(
    u_left, u_right, s_left, s_right, j_left, j_right, rotor, to_left, to_right, *, pairs, tiles, blocks
):
    even16 = checker(16)
    lane = lax.broadcasted_iota(jnp.int32, (16, LANES), 1)

    def block_cols(q, _):
        rows = pl.ds(pl.multiple_of(16 * q, 16), 16)
        for c in range(tiles):
            panel = rotor[rows, c * LANES : (c + 1) * LANES]
            to_left[2 * blocks + q * tiles + c] = panel
            to_right[2 * blocks + q * tiles + c] = panel
        for refs, out_ref, red_first in (
            ((u_left, s_left, j_left), to_left, False),
            ((u_right, s_right, j_right), to_right, True),
        ):
            packed = []
            for ref in refs:
                acc = [jnp.zeros((8, LANES), jnp.float32)]
                total = acc[0]
                for m in range(pairs):
                    first = f32(ref[2 * m, rows, :])
                    second = f32(ref[2 * m + 1, rows, :])
                    red = jnp.where(even16, first, second)
                    black = jnp.where(even16, second, first)
                    for w in (0, 1):
                        g = m + pairs * w
                        near = pltpu.roll(red[8 * w : 8 * w + 8], (8 * g + 4) % LANES, 1)
                        far = pltpu.roll(black[8 * w : 8 * w + 8], (8 * g + 8) % LANES, 1)
                        if red_first:
                            near_slot, far_slot = 8 * g, 8 * g + 4
                        else:
                            near_slot, far_slot = 8 * g + 4, (8 * g + 8) % LANES
                        l8 = lane[:8]
                        total = jnp.where((l8 >= near_slot) & (l8 < near_slot + 4), near, total)
                        total = jnp.where((l8 >= far_slot) & (l8 < far_slot + 4), far, total)
                packed.append(total)
            high, low = split_high_low(packed[0])
            out_ref[2 * q] = jnp.concatenate([high, low], 0).astype(jnp.bfloat16)
            out_ref[2 * q + 1] = jnp.concatenate([packed[1], packed[2]], 0).astype(jnp.bfloat16)
        return 0

    lax.fori_loop(0, blocks, block_cols, 0)


def whole_at(shape, index):
    return pl.BlockSpec(shape, lambda i: index)


def pack_rows(field, sigma, current):
    layers, rows, cols = field.shape
    pairs, tiles = layers // 2, cols // LANES

    def row_specs(height):
        shape = (layers, height, cols)
        return [whole_at(shape, (0, 0, 0)), whole_at(shape, (0, rows // height - 1, 0))]

    shape = (2, pairs, 16, cols)
    return pl.pallas_call(
        functools.partial(rows_kernel, pairs=pairs, tiles=tiles),
        grid=(1,),
        in_specs=row_specs(8) + row_specs(16) * 2,
        out_specs=[whole_at(shape, (0,) * 4)] * 2,
        out_shape=[jax.ShapeDtypeStruct(shape, jnp.bfloat16)] * 2,
        compiler_params=pltpu.CompilerParams(vmem_limit_bytes=VMEM_BYTES),
        cost_estimate=pl.CostEstimate(flops=0, bytes_accessed=12 << 20, transcendentals=0),
        name="pack_rows",
    )(field, field, sigma, sigma, current, current)


def pack_cols(field, sigma, current, rotor_cycle):
    layers, rows, cols = field.shape
    pairs, tiles, blocks = layers // 2, cols // LANES, rows // 16
    shape = (layers, rows, LANES)
    col_specs = [whole_at(shape, (0, 0, 0)), whole_at(shape, (0, 0, tiles - 1))]
    out = (blocks * (tiles + 2), 16, LANES)
    return pl.pallas_call(
        functools.partial(cols_kernel, pairs=pairs, tiles=tiles, blocks=blocks),
        grid=(1,),
        in_specs=col_specs * 3 + [whole_at((rows, cols), (0, 0))],
        out_specs=[whole_at(out, (0,) * 3)] * 2,
        out_shape=[jax.ShapeDtypeStruct(out, jnp.bfloat16)] * 2,
        compiler_params=pltpu.CompilerParams(vmem_limit_bytes=VMEM_BYTES),
        cost_estimate=pl.CostEstimate(flops=0, bytes_accessed=16 << 20, transcendentals=0),
        name="pack_cols",
    )(field, field, sigma, sigma, current, current, rotor_cycle)


def place_kernel(*refs, slots, rows, tiles):
    rotor = refs[: slots - 2]
    skew, from_left, from_right, placed_ref, small_prev, small_next = refs[slots - 2 :]
    blocks = rows // 16
    lane16 = lax.broadcasted_iota(jnp.int32, (16, LANES), 1)
    panels = slots * tiles
    bits = (panels - 1).bit_length()
    want = [(panels - tiles - 1 + p) % panels for p in range(tiles + 2)]
    needs = [set(want)]
    for bit in range(bits):
        needs.append(needs[-1] | {(q - (1 << bit)) % panels for q in needs[-1]})

    def rotor_rows(b, _):
        at = pl.ds(pl.multiple_of(16 * b, 16), 16)
        turn = skew[at, :]

        def panel(steps, c):
            if steps in (1, slots - 1):
                source = from_left if steps == 1 else from_right
                return source[2 * blocks + b * tiles + c]
            source = rotor[0] if steps == 0 else rotor[steps - 1]
            return source[at, c * LANES : (c + 1) * LANES]

        cur = {q: f32(panel(slots - 1 - q // tiles, q % tiles)) for q in sorted(needs[bits])}
        for bit in reversed(range(bits)):
            on = ((turn >> bit) & 1) == 1
            cur = {q: jnp.where(on, cur[(q - (1 << bit)) % panels], cur[q]) for q in sorted(needs[bit])}
        for p in range(tiles):
            placed_ref[p, at, :] = cur[want[p + 1]].astype(jnp.bfloat16)
        side = jnp.where(lane16 < LANES // 2, cur[want[tiles + 1]], cur[want[0]])
        placed_ref[tiles, at, :] = side.astype(jnp.bfloat16)
        return 0

    lax.fori_loop(0, rows // 16, rotor_rows, 0)
    for out_ref, corner, first in (
        (small_prev, 0, 0),
        (small_next, 2 * blocks - 2, rows - 16),
    ):
        for i in (0, 1):
            out_ref[i] = from_left[corner + i]
            out_ref[2 + i] = from_right[corner + i]
        for c in range(tiles + 1):
            out_ref[4 + c] = placed_ref[c, first : first + 16, :]


def place_cycle(rotor, skew, from_left, from_right):
    rows, cols = rotor[0].shape
    tiles = cols // LANES
    sides = whole_at(from_left.shape, (0, 0, 0))
    out = [(tiles + 1, rows, LANES)] + [(tiles + 5, 16, LANES)] * 2
    return pl.pallas_call(
        functools.partial(place_kernel, slots=len(rotor) + 2, rows=rows, tiles=tiles),
        grid=(1,),
        in_specs=[whole_at((rows, cols), (0, 0))] * len(rotor) + [whole_at((rows, LANES), (0, 0)), sides, sides],
        out_specs=[whole_at(x, (0,) * 3) for x in out],
        out_shape=[jax.ShapeDtypeStruct(x, jnp.bfloat16) for x in out],
        compiler_params=pltpu.CompilerParams(vmem_limit_bytes=VMEM_BYTES),
        cost_estimate=pl.CostEstimate(flops=0, bytes_accessed=4 << 20, transcendentals=0),
        name="place_cycle",
    )(*rotor, skew, from_left, from_right)


def relax_kernel(placed, small_prev, small_next, from_left, from_right, from_prev, from_next,
     u_ref, s_ref, j_ref, out_ref,
     red_a, red_b, black_a, black_b, sig_r, sig_b, cur_r, cur_b, side, *, pairs, rows, tiles):
    g = pl.program_id(0)
    blocks = rows // 16
    even8 = checker(8)
    even16 = checker(16)
    lane = lax.broadcasted_iota(jnp.int32, (8, LANES), 1)
    lane_first = lane == 0
    lane_last = lane == LANES - 1

    @pl.when(g == 0)
    def prologue():
        def fill(value, c, spots):
            zero = jnp.zeros((8, LANES), jnp.float32)
            for buf in (red_a, red_b, black_a, black_b):
                for half, to in spots:
                    buf[0, c, to, :] = value[8 * half : 8 * half + 8]
                    buf[pairs + 1, c, to, :] = zero

        def placed_rows(b, _):
            at = pl.ds(pl.multiple_of(16 * b, 16), 16)
            spots = [(half, pl.ds(pl.multiple_of(16 * b + EDGE + 8 * half, 8), 8)) for half in (0, 1)]
            for c in range(tiles + 1):
                fill(f32(placed[c, at, :]), c, spots)
            return 0

        lax.fori_loop(0, blocks, placed_rows, 0)
        for c in range(tiles + 1):
            fill(f32(small_prev[4 + c]), c, [(1, pl.ds(0, 8))])
            fill(f32(small_next[4 + c]), c, [(0, pl.ds(EDGE + rows, 8))])

        left_slot = (lane & 7) < 4

        def decode(q, left, right):
            left0, left1, right0, right1 = f32(left[0]), f32(left[1]), f32(right[0]), f32(right[1])
            items = (
                (left0[:8] + left0[8:], right0[:8] + right0[8:], 1.0),
                (left1[:8], right1[:8], 1.0 / 48.0),
                (left1[8:], right1[8:], 0.25),
            )
            for item, (a, b, scale) in enumerate(items):
                side[0, item, q] = jnp.where(left_slot, a, b) * scale
                side[1, item, q] = jnp.where(left_slot, b, a) * scale

        for q in range(blocks):
            pick = slice(2 * q, 2 * q + 2)
            decode(q, from_left[pick], from_right[pick])
        decode(blocks, small_prev[0:2], small_prev[2:4])
        decode(blocks + 1, small_next[0:2], small_next[2:4])

    @pl.when(g < pairs)
    def load():
        m = g
        fields = ((red_a, sig_r, cur_r), (black_a, sig_b, cur_b))
        for colour in (0, 1):
            u_dst, s_dst, j_dst = fields[colour]
            for c in range(tiles):
                cols = slice(c * LANES, (c + 1) * LANES)
                both = f32(from_prev[colour, 0, :, cols])
                u_dst[m + 1, c, pl.ds(EDGE - 5, 8), :] = both[:8] + both[8:]
                s_dst[m, c, pl.ds(0, 8), :] = both[:8] * (1.0 / 48.0)
                j_dst[m, c, pl.ds(0, 8), :] = both[8:] * 0.25
                both = f32(from_next[colour, 0, :, cols])
                u_dst[m + 1, c, pl.ds(EDGE + rows, 8), :] = both[:8] + both[8:]
                s_dst[m, c, pl.ds(EDGE + rows - 5, 8), :] = both[:8] * (1.0 / 48.0)
                j_dst[m, c, pl.ds(EDGE + rows - 5, 8), :] = both[8:] * 0.25

        def own_rows(q, _):
            at = pl.ds(pl.multiple_of(16 * q, 16), 16)
            to = pl.ds(pl.multiple_of(16 * q + EDGE, 8), 16)
            for c in range(tiles):
                cols = slice(c * LANES, (c + 1) * LANES)
                a, b = u_ref[0, at, cols], u_ref[1, at, cols]
                red_a[m + 1, c, to, :] = jnp.where(even16, a, b)
                black_a[m + 1, c, to, :] = jnp.where(even16, b, a)
                a, b = f32(s_ref[0, at, cols]) * (1.0 / 48.0), f32(s_ref[1, at, cols]) * (1.0 / 48.0)
                sig_r[m, c, to, :] = jnp.where(even16, a, b)
                sig_b[m, c, to, :] = jnp.where(even16, b, a)
                a, b = f32(j_ref[0, at, cols]) * 0.25, f32(j_ref[1, at, cols]) * 0.25
                cur_r[m, c, to, :] = jnp.where(even16, a, b)
                cur_b[m, c, to, :] = jnp.where(even16, b, a)
            return 0

        lax.fori_loop(0, blocks, own_rows, 0)

        for colour in (0, 1):
            u_dst, s_dst, j_dst = fields[colour]
            for item, (dst, plane) in enumerate(((u_dst, m + 1), (s_dst, m), (j_dst, m))):
                for w in (0, 1):
                    turn = lax.rem(2 * LANES + 124 - 4 * colour - 8 * (m + pairs * w), LANES)
                    for q in range(blocks):
                        dst[plane, tiles, pl.ds(EDGE + 16 * q + 8 * w, 8), :] = pltpu.roll(side[colour, item, q], turn, 1)
                    if w == 1:
                        dst[plane, tiles, pl.ds(0, 8), :] = pltpu.roll(side[colour, item, blocks], turn, 1)
                    else:
                        dst[plane, tiles, pl.ds(EDGE + rows, 8), :] = pltpu.roll(side[colour, item, blocks + 1], turn, 1)

    def half_step(m, colour, own, other, sig, cur, start, stride, outputs, write):
        def row_tile(at):
            centre = [other[m + 1, c, pl.ds(at, 8), :] for c in range(tiles + 1)]
            ahead = [pltpu.roll(x, 1, 1) for x in centre]
            back = [pltpu.roll(x, LANES - 1, 1) for x in centre]
            for c in range(outputs):
                left = jnp.where(lane_first, ahead[c - 1], ahead[c])
                right = jnp.where(lane_last, back[(c + 1) % (tiles + 1)], back[c])
                below = other[m, c, pl.ds(at, 8), :]
                above = other[m + 2, c, pl.ds(at, 8), :]
                outer = jnp.where(even8, below, above) if colour == 0 else jnp.where(even8, above, below)
                near = other[m + 1, c, pl.ds(at + 1, 8), :] - other[m + 1, c, pl.ds(at - 1, 8), :]
                far = own[m + 1, c, pl.ds(at + 2, 8), :] - own[m + 1, c, pl.ds(at - 2, 8), :]
                total = (left + right) + (centre[c] + outer)
                new = cur[m, c, pl.ds(at, 8), :] + 0.25 * total - sig[m, c, pl.ds(at, 8), :] * (8.0 * near - far)
                write(m, c, at, new)

        def body(r, _):
            for k in range(UNROLL):
                row_tile(start + stride * r + 8 * k)
            return 0

        lax.fori_loop(0, SPANS, body, 0)

    def keep(buf):
        def write(m, c, at, new):
            buf[m + 1, c, pl.ds(at, 8), :] = new

        return write

    def emit(m, c, at, new):
        red = red_a[m + 1, c, pl.ds(at, 8), :]
        cols = slice(c * LANES, (c + 1) * LANES)
        to = pl.ds(pl.multiple_of(at - EDGE, 8), 8)
        out_ref[0, to, cols] = jnp.where(even8, red, new)
        out_ref[1, to, cols] = jnp.where(even8, new, red)

    window = 8 * UNROLL
    wide = (EDGE - 4, (rows + 8 - window) // (SPANS - 1), tiles + 1)
    last = (EDGE, (rows - window) // (SPANS - 1), tiles)
    plan = (
        (1, 0, red_a, black_a, sig_r, cur_r, wide, keep(red_b)),
        (2, 1, black_a, red_b, sig_b, cur_b, wide, keep(black_b)),
        (3, 0, red_b, black_b, sig_r, cur_r, wide, keep(red_a)),
        (4, 1, black_b, red_a, sig_b, cur_b, last, emit),
    )
    for lag, colour, own, other, sig, cur, where, write in plan:

        @pl.when((g >= lag) & (g < pairs + lag))
        def phase(lag=lag, colour=colour, own=own, other=other, sig=sig, cur=cur, where=where, write=write):
            half_step(g - lag, colour, own, other, sig, cur, *where, write)


def relax(placed, small_prev, small_next, from_left, from_right, from_prev, from_next, field, sigma, current):
    layers, rows, cols = field.shape
    pairs, tiles = layers // 2, cols // LANES
    ext = rows + 2 * EDGE

    def whole(array):
        zeros = (0,) * array.ndim
        return pl.BlockSpec(array.shape, lambda g: zeros)

    def coming(g):
        return jnp.minimum(g, pairs - 1)

    halo = pl.BlockSpec((2, 1, 16, cols), lambda g: (0, coming(g), 0, 0))
    block = pl.BlockSpec((2, rows, cols), lambda g: (coming(g), 0, 0))
    fixed = [placed, small_prev, small_next]
    side = pl.BlockSpec((rows // 8, 16, LANES), lambda g: (0, 0, 0))
    state = pltpu.VMEM((pairs + 2, tiles + 1, ext, LANES), jnp.float32)
    coef = pltpu.VMEM((pairs, tiles + 1, ext, LANES), jnp.float32)
    return pl.pallas_call(
        functools.partial(relax_kernel, pairs=pairs, rows=rows, tiles=tiles),
        grid=(pairs + LAG,),
        in_specs=[whole(a) for a in fixed] + [side, side, halo, halo, block, block, block],
        out_specs=pl.BlockSpec((2, rows, cols), lambda g: (jnp.maximum(g - LAG, 0), 0, 0)),
        out_shape=jax.ShapeDtypeStruct(field.shape, jnp.float32),
        scratch_shapes=[state] * 4 + [coef] * 4 + [pltpu.VMEM((2, 3, rows // 16 + 2, 8, LANES), jnp.float32)],
        compiler_params=pltpu.CompilerParams(vmem_limit_bytes=VMEM_BYTES),
        name="relax",
    )(*fixed, from_left, from_right, from_prev, from_next, field, sigma, current)


def moved(value, axis, steps):
    count = lax.axis_size(axis)
    return lax.ppermute(value, axis, [(i, (i + steps) % count) for i in range(count)])


def local(field, sigma, current, rotor_cycle, skew_list):
    rows = field.shape[1]
    skew = jnp.broadcast_to(skew_list[:, None], (rows, LANES))
    rotor = [rotor_cycle] + [moved(rotor_cycle, "az", s) for s in range(2, lax.axis_size("az") - 1)]
    to_left, to_right = pack_cols(field, sigma, current, rotor_cycle)
    from_left, from_right = moved(to_right, "az", 1), moved(to_left, "az", -1)
    to_prev, to_next = pack_rows(field, sigma, current)
    from_prev, from_next = moved(to_next, "ta", 1), moved(to_prev, "ta", -1)
    placed, small_to_prev, small_to_next = place_cycle(rotor, skew, from_left, from_right)
    small_prev, small_next = moved(small_to_next, "ta", 1), moved(small_to_prev, "ta", -1)
    return relax(
        placed, small_prev, small_next, from_left, from_right, from_prev, from_next, field, sigma, current
    )


def solution(mesh):
    placed = (P(None, "ta", "az"), P(None, "ta", "az"), P(None, "ta", "az"), P("ta", "az"), P("ta"))
    return jax.shard_map(
        local, mesh=mesh, in_specs=placed, out_specs=P(None, "ta", "az"), check_vma=False
    )
```

```python
import functools

import jax
import jax.numpy as jnp
from jax import lax
from jax.experimental import pallas as pl
from jax.experimental.pallas import tpu as pltpu
from jax.sharding import PartitionSpec as P

LANES = 128
EDGE = 8
LAG = 4
VMEM_BYTES = 60 * 1024 * 1024


def checker(rows):
    sub = lax.broadcasted_iota(jnp.int32, (rows, LANES), 0)
    lane = lax.broadcasted_iota(jnp.int32, (rows, LANES), 1)
    return ((sub + lane) & 1) == 0


def f32(value):
    return value.astype(jnp.float32)


def split_high_low(value):
    high = f32(value.astype(jnp.bfloat16))
    return high, value - high


def rows_kernel(u_top, u_bot, s_top, s_bot, j_top, j_bot, after, to_prev, to_next, *, pairs, tiles):
    even8 = checker(8)
    sub = lax.broadcasted_iota(jnp.int32, (8, LANES), 0)
    field_rows = sub < 5

    def pair_rows(m, _):
        for c in range(tiles):
            cols = slice(c * LANES, (c + 1) * LANES)
            for u_ref, s_ref, j_ref, half, out_ref in (
                (u_top, s_top, j_top, 0, to_prev),
                (u_bot, s_bot, j_bot, 8, to_next),
            ):
                eo = []
                for ref in (u_ref, s_ref, j_ref):
                    first = f32(ref[2 * m, :, cols])
                    second = f32(ref[2 * m + 1, :, cols])
                    if first.shape[0] == 16:
                        first = first[half : half + 8]
                        second = second[half : half + 8]
                    eo.append((first, second))
                for colour in (0, 1):
                    pick = [
                        jnp.where(even8, a, b) if colour == 0 else jnp.where(even8, b, a)
                        for a, b in eo
                    ]
                    high, low = split_high_low(pick[0])
                    sig, cur = pick[1], pick[2]
                    if half == 0:
                        sig = pltpu.roll(sig, 5, 0)
                        cur = pltpu.roll(cur, 5, 0)
                    else:
                        high = pltpu.roll(high, 5, 0)
                        low = pltpu.roll(low, 5, 0)
                    both = jnp.concatenate(
                        [jnp.where(field_rows, high, sig), jnp.where(field_rows, low, cur)], 0
                    )
                    out_ref[colour, m, :, cols] = both.astype(jnp.bfloat16)
        return 0

    lax.fori_loop(0, pairs, pair_rows, 0)


def cols_kernel(
    u_left, u_right, s_left, s_right, j_left, j_right, rotor, to_left, to_right, *, pairs, tiles, blocks
):
    even16 = checker(16)
    slot = lax.broadcasted_iota(jnp.int32, (8, LANES), 1) // 4
    slots = LANES // 4
    for q in range(blocks):
        rows = slice(16 * q, 16 * q + 16)
        for c in range(tiles):
            panel = rotor[rows, c * LANES : (c + 1) * LANES]
            to_left[q, 2 + c] = panel
            to_right[q, 2 + c] = panel
        for refs, out_ref, near_at, far_at in (
            ((u_left, s_left, j_left), to_left, 1, 2),
            ((u_right, s_right, j_right), to_right, 0, 1),
        ):
            packed = []
            for ref in refs:
                total = jnp.zeros((8, LANES), jnp.float32)
                for m in range(pairs):
                    first = f32(ref[2 * m, rows, :])
                    second = f32(ref[2 * m + 1, rows, :])
                    red = jnp.where(even16, first, second)
                    black = jnp.where(even16, second, first)
                    for w in (0, 1):
                        g = m + pairs * w
                        near = pltpu.roll(red[8 * w : 8 * w + 8], (8 * g + 4) % LANES, 1)
                        far = pltpu.roll(black[8 * w : 8 * w + 8], (8 * g + 8) % LANES, 1)
                        total = jnp.where(slot == (2 * g + near_at) % slots, near, total)
                        total = jnp.where(slot == (2 * g + far_at) % slots, far, total)
                packed.append(total)
            high, low = split_high_low(packed[0])
            out_ref[q, 0] = jnp.concatenate([high, low], 0).astype(jnp.bfloat16)
            out_ref[q, 1] = jnp.concatenate([packed[1], packed[2]], 0).astype(jnp.bfloat16)


def whole_at(shape, index):
    return pl.BlockSpec(shape, lambda i: index)


def pack_rows(field, sigma, current, after):
    layers, rows, cols = field.shape
    pairs, tiles = layers // 2, cols // LANES

    def row_specs(height):
        shape = (layers, height, cols)
        return [whole_at(shape, (0, 0, 0)), whole_at(shape, (0, rows // height - 1, 0))]

    shape = (2, pairs, 16, cols)
    return pl.pallas_call(
        functools.partial(rows_kernel, pairs=pairs, tiles=tiles),
        grid=(1,),
        in_specs=row_specs(8) + row_specs(16) * 2 + [pl.BlockSpec(memory_space=pl.ANY)],
        out_specs=[whole_at(shape, (0,) * 4)] * 2,
        out_shape=[jax.ShapeDtypeStruct(shape, jnp.bfloat16)] * 2,
        compiler_params=pltpu.CompilerParams(vmem_limit_bytes=VMEM_BYTES),
        cost_estimate=pl.CostEstimate(flops=0, bytes_accessed=12 << 20, transcendentals=0),
        name="pack_rows",
    )(field, field, sigma, sigma, current, current, after)


def pack_cols(field, sigma, current, rotor_cycle):
    layers, rows, cols = field.shape
    pairs, tiles, blocks = layers // 2, cols // LANES, rows // 16
    part = 2
    shape = (layers, 16 * part, LANES)
    col_specs = [pl.BlockSpec(shape, lambda i: (0, i, 0)), pl.BlockSpec(shape, lambda i: (0, i, tiles - 1))]
    out_spec = pl.BlockSpec((part, tiles + 2, 16, LANES), lambda i: (i, 0, 0, 0))
    return pl.pallas_call(
        functools.partial(cols_kernel, pairs=pairs, tiles=tiles, blocks=part),
        grid=(blocks // part,),
        in_specs=col_specs * 3 + [pl.BlockSpec((16 * part, cols), lambda i: (i, 0))],
        out_specs=[out_spec] * 2,
        out_shape=[jax.ShapeDtypeStruct((blocks, tiles + 2, 16, LANES), jnp.bfloat16)] * 2,
        compiler_params=pltpu.CompilerParams(vmem_limit_bytes=VMEM_BYTES),
        cost_estimate=pl.CostEstimate(flops=0, bytes_accessed=16 << 20, transcendentals=0),
        name="pack_cols",
    )(field, field, sigma, sigma, current, current, rotor_cycle)


def place_block(row, skew, rotor, from_left, from_right, at, slots, tiles):
    lane16 = lax.broadcasted_iota(jnp.int32, (16, LANES), 1)
    sub16 = lax.broadcasted_iota(jnp.int32, (16, LANES), 0)
    panels = slots * tiles
    bits = (panels - 1).bit_length()
    want = [(panels - tiles - 1 + p) % panels for p in range(tiles + 2)]
    needs = [set(want)]
    for bit in range(bits):
        needs.append(needs[-1] | {(q - (1 << bit)) % panels for q in needs[-1]})
    turn = jnp.zeros((16, LANES), jnp.int32)
    for i in range(16):
        turn = jnp.where(sub16 == i, skew[row + i], turn)

    def panel(steps, c):
        if steps in (1, slots - 1):
            return (from_left if steps == 1 else from_right)[at, 2 + c]
        source = rotor[0] if steps == 0 else rotor[steps - 1]
        return source[pl.ds(pl.multiple_of(16 * at, 16), 16), c * LANES : (c + 1) * LANES]

    cur = {q: f32(panel(slots - 1 - q // tiles, q % tiles)) for q in sorted(needs[bits])}
    for bit in reversed(range(bits)):
        on = ((turn >> bit) & 1) == 1
        cur = {q: jnp.where(on, cur[(q - (1 << bit)) % panels], cur[q]) for q in sorted(needs[bit])}
    placed = [cur[want[p + 1]] for p in range(tiles)]
    placed.append(jnp.where(lane16 < LANES // 2, cur[want[tiles + 1]], cur[want[0]]))
    return [x.astype(jnp.bfloat16) for x in placed]


def place_edges_kernel(skew, *refs, slots, rows, tiles):
    near, far, outs = refs[:slots], refs[slots : 2 * slots], refs[2 * slots :]
    for out_ref, ins, row in ((outs[0], near, 0), (outs[1], far, rows - 16)):
        from_left, from_right = ins[slots - 2 :]
        for i in (0, 1):
            out_ref[i] = from_left[0, i]
            out_ref[2 + i] = from_right[0, i]
        for c, value in enumerate(place_block(row, skew, ins[: slots - 2], from_left, from_right, 0, slots, tiles)):
            out_ref[4 + c] = value


def place_edges(rotor, skew_list, from_left, from_right):
    rows, cols = rotor[0].shape
    tiles, slots, blocks = cols // LANES, len(rotor) + 2, rows // 16

    def specs(i):
        side = whole_at((1, tiles + 2, 16, LANES), (i, 0, 0, 0))
        return [whole_at((16, cols), (i, 0))] * len(rotor) + [side, side]

    out = (tiles + 5, 16, LANES)
    ins = [*rotor, from_left, from_right]
    return pl.pallas_call(
        functools.partial(place_edges_kernel, slots=slots, rows=rows, tiles=tiles),
        grid=(1,),
        in_specs=[pl.BlockSpec(memory_space=pltpu.SMEM)] + specs(0) + specs(blocks - 1),
        out_specs=[whole_at(out, (0,) * 3)] * 2,
        out_shape=[jax.ShapeDtypeStruct(out, jnp.bfloat16)] * 2,
        compiler_params=pltpu.CompilerParams(vmem_limit_bytes=VMEM_BYTES),
        cost_estimate=pl.CostEstimate(flops=0, bytes_accessed=1 << 20, transcendentals=0),
        name="place_edges",
    )(skew_list, *ins, *ins)


def place_kernel(skew, *refs, slots, rows, tiles):
    rotor = refs[: slots - 2]
    from_left, from_right, after, placed_ref = refs[slots - 2 :]

    def rotor_rows(b, _):
        at = pl.ds(pl.multiple_of(16 * b, 16), 16)
        for p, value in enumerate(place_block(16 * b, skew, rotor, from_left, from_right, b, slots, tiles)):
            placed_ref[p, at, :] = value
        return 0

    lax.fori_loop(0, rows // 16, rotor_rows, 0)


def place_cycle(rotor, skew_list, from_left, from_right, after):
    rows, cols = rotor[0].shape
    tiles = cols // LANES
    sides = whole_at(from_left.shape, (0, 0, 0, 0))
    out = (tiles + 1, rows, LANES)
    return pl.pallas_call(
        functools.partial(place_kernel, slots=len(rotor) + 2, rows=rows, tiles=tiles),
        grid=(1,),
        in_specs=[pl.BlockSpec(memory_space=pltpu.SMEM)]
        + [whole_at((rows, cols), (0, 0))] * len(rotor)
        + [sides, sides, pl.BlockSpec(memory_space=pl.ANY)],
        out_specs=whole_at(out, (0,) * 3),
        out_shape=jax.ShapeDtypeStruct(out, jnp.bfloat16),
        compiler_params=pltpu.CompilerParams(vmem_limit_bytes=VMEM_BYTES),
        cost_estimate=pl.CostEstimate(flops=0, bytes_accessed=4 << 20, transcendentals=0),
        name="place_cycle",
    )(skew_list, *rotor, from_left, from_right, after)


def relax_kernel(placed, small_prev, small_next, from_left, from_right, from_prev, from_next,
     u_ref, s_ref, j_ref, out_ref,
     red_a, red_b, black_a, black_b, sig_r, sig_b, cur_r, cur_b, side, *, pairs, rows, tiles):
    g = pl.program_id(0)
    blocks = rows // 16
    even8 = checker(8)
    even16 = checker(16)
    lane = lax.broadcasted_iota(jnp.int32, (8, LANES), 1)
    lane_first = lane == 0
    lane_last = lane == LANES - 1

    @pl.when(g == 0)
    def prologue():
        def fill(value, c, spots):
            zero = jnp.zeros((8, LANES), jnp.float32)
            for buf in (red_a, red_b, black_a, black_b):
                for half, to in spots:
                    buf[0, c, to, :] = value[8 * half : 8 * half + 8]
                    buf[pairs + 1, c, to, :] = zero

        def placed_rows(b, _):
            at = pl.ds(pl.multiple_of(16 * b, 16), 16)
            spots = [(half, pl.ds(pl.multiple_of(16 * b + EDGE + 8 * half, 8), 8)) for half in (0, 1)]
            for c in range(tiles + 1):
                fill(f32(placed[c, at, :]), c, spots)
            return 0

        lax.fori_loop(0, blocks, placed_rows, 0)
        for c in range(tiles + 1):
            fill(f32(small_prev[4 + c]), c, [(1, pl.ds(0, 8))])
            fill(f32(small_next[4 + c]), c, [(0, pl.ds(EDGE + rows, 8))])

        left_slot = (lane & 7) < 4

        def decode(q, left, right):
            left0, left1, right0, right1 = f32(left[0]), f32(left[1]), f32(right[0]), f32(right[1])
            items = (
                (left0[:8] + left0[8:], right0[:8] + right0[8:], 1.0),
                (left1[:8], right1[:8], 1.0 / 48.0),
                (left1[8:], right1[8:], 0.25),
            )
            for item, (a, b, scale) in enumerate(items):
                side[0, item, q] = jnp.where(left_slot, a, b) * scale
                side[1, item, q] = jnp.where(left_slot, b, a) * scale

        for q in range(blocks):
            decode(q, from_left[q], from_right[q])
        decode(blocks, small_prev[0:2], small_prev[2:4])
        decode(blocks + 1, small_next[0:2], small_next[2:4])

    @pl.when(g < pairs)
    def load():
        m = g
        fields = ((red_a, sig_r, cur_r), (black_a, sig_b, cur_b))
        for colour in (0, 1):
            u_dst, s_dst, j_dst = fields[colour]
            for c in range(tiles):
                cols = slice(c * LANES, (c + 1) * LANES)
                both = f32(from_prev[colour, 0, :, cols])
                u_dst[m + 1, c, pl.ds(EDGE - 5, 8), :] = both[:8] + both[8:]
                s_dst[m, c, pl.ds(0, 8), :] = both[:8] * (1.0 / 48.0)
                j_dst[m, c, pl.ds(0, 8), :] = both[8:] * 0.25
                both = f32(from_next[colour, 0, :, cols])
                u_dst[m + 1, c, pl.ds(EDGE + rows, 8), :] = both[:8] + both[8:]
                s_dst[m, c, pl.ds(EDGE + rows - 5, 8), :] = both[:8] * (1.0 / 48.0)
                j_dst[m, c, pl.ds(EDGE + rows - 5, 8), :] = both[8:] * 0.25

        def own_rows(q, _):
            at = pl.ds(pl.multiple_of(16 * q, 16), 16)
            to = pl.ds(pl.multiple_of(16 * q + EDGE, 8), 16)
            for c in range(tiles):
                cols = slice(c * LANES, (c + 1) * LANES)
                a, b = u_ref[0, at, cols], u_ref[1, at, cols]
                red_a[m + 1, c, to, :] = jnp.where(even16, a, b)
                black_a[m + 1, c, to, :] = jnp.where(even16, b, a)
                a, b = f32(s_ref[0, at, cols]) * (1.0 / 48.0), f32(s_ref[1, at, cols]) * (1.0 / 48.0)
                sig_r[m, c, to, :] = jnp.where(even16, a, b)
                sig_b[m, c, to, :] = jnp.where(even16, b, a)
                a, b = f32(j_ref[0, at, cols]) * 0.25, f32(j_ref[1, at, cols]) * 0.25
                cur_r[m, c, to, :] = jnp.where(even16, a, b)
                cur_b[m, c, to, :] = jnp.where(even16, b, a)
            return 0

        lax.fori_loop(0, blocks, own_rows, 0)

        for colour in (0, 1):
            u_dst, s_dst, j_dst = fields[colour]
            for item, (dst, plane) in enumerate(((u_dst, m + 1), (s_dst, m), (j_dst, m))):
                for w in (0, 1):
                    turn = lax.rem(2 * LANES + 124 - 4 * colour - 8 * (m + pairs * w), LANES)
                    for q in range(blocks):
                        dst[plane, tiles, pl.ds(EDGE + 16 * q + 8 * w, 8), :] = pltpu.roll(side[colour, item, q], turn, 1)
                    if w == 1:
                        dst[plane, tiles, pl.ds(0, 8), :] = pltpu.roll(side[colour, item, blocks], turn, 1)
                    else:
                        dst[plane, tiles, pl.ds(EDGE + rows, 8), :] = pltpu.roll(side[colour, item, blocks + 1], turn, 1)

    def half_step(m, colour, own, other, sig, cur, start, count, outputs, write):
        def row_tile(at):
            centre = [other[m + 1, c, pl.ds(at, 8), :] for c in range(tiles + 1)]
            ahead = [pltpu.roll(x, 1, 1) for x in centre]
            back = [pltpu.roll(x, LANES - 1, 1) for x in centre]
            for c in range(outputs):
                left = jnp.where(lane_first, ahead[c - 1], ahead[c])
                right = jnp.where(lane_last, back[(c + 1) % (tiles + 1)], back[c])
                below = other[m, c, pl.ds(at, 8), :]
                above = other[m + 2, c, pl.ds(at, 8), :]
                outer = jnp.where(even8, below, above) if colour == 0 else jnp.where(even8, above, below)
                near = other[m + 1, c, pl.ds(at + 1, 8), :] - other[m + 1, c, pl.ds(at - 1, 8), :]
                far = own[m + 1, c, pl.ds(at + 2, 8), :] - own[m + 1, c, pl.ds(at - 2, 8), :]
                total = (left + right) + (centre[c] + outer)
                new = cur[m, c, pl.ds(at, 8), :] + 0.25 * total - sig[m, c, pl.ds(at, 8), :] * (8.0 * near - far)
                write(m, c, at, new)

        for r in range(count):
            row_tile(start + 8 * r)

    def keep(buf):
        def write(m, c, at, new):
            buf[m + 1, c, pl.ds(at, 8), :] = new

        return write

    def emit(m, c, at, new):
        red = red_a[m + 1, c, pl.ds(at, 8), :]
        cols = slice(c * LANES, (c + 1) * LANES)
        to = pl.ds(pl.multiple_of(at - EDGE, 8), 8)
        out_ref[0, to, cols] = jnp.where(even8, red, new)
        out_ref[1, to, cols] = jnp.where(even8, new, red)

    wide = (EDGE - 4, rows // 8 + 1, tiles + 1)
    last = (EDGE, rows // 8, tiles)
    plan = (
        (1, 0, red_a, black_a, sig_r, cur_r, wide, keep(red_b)),
        (2, 1, black_a, red_b, sig_b, cur_b, wide, keep(black_b)),
        (3, 0, red_b, black_b, sig_r, cur_r, wide, keep(red_a)),
        (4, 1, black_b, red_a, sig_b, cur_b, last, emit),
    )
    for lag, colour, own, other, sig, cur, where, write in plan:

        @pl.when((g >= lag) & (g < pairs + lag))
        def phase(lag=lag, colour=colour, own=own, other=other, sig=sig, cur=cur, where=where, write=write):
            half_step(g - lag, colour, own, other, sig, cur, *where, write)


def relax(placed, small_prev, small_next, from_left, from_right, from_prev, from_next, field, sigma, current):
    layers, rows, cols = field.shape
    pairs, tiles = layers // 2, cols // LANES
    ext = rows + 2 * EDGE

    def whole(array):
        zeros = (0,) * array.ndim
        return pl.BlockSpec(array.shape, lambda g: zeros)

    def coming(g):
        return jnp.minimum(g, pairs - 1)

    halo = pl.BlockSpec((2, 1, 16, cols), lambda g: (0, coming(g), 0, 0))
    block = pl.BlockSpec((2, rows, cols), lambda g: (coming(g), 0, 0))
    fixed = [placed, small_prev, small_next]
    side = pl.BlockSpec((rows // 16, 2, 16, LANES), lambda g: (0, 0, 0, 0))
    state = pltpu.VMEM((pairs + 2, tiles + 1, ext, LANES), jnp.float32)
    coef = pltpu.VMEM((pairs, tiles + 1, ext, LANES), jnp.float32)
    return pl.pallas_call(
        functools.partial(relax_kernel, pairs=pairs, rows=rows, tiles=tiles),
        grid=(pairs + LAG,),
        in_specs=[whole(a) for a in fixed] + [side, side, halo, halo, block, block, block],
        out_specs=pl.BlockSpec((2, rows, cols), lambda g: (jnp.maximum(g - LAG, 0), 0, 0)),
        out_shape=jax.ShapeDtypeStruct(field.shape, jnp.float32),
        scratch_shapes=[state] * 4 + [coef] * 4 + [pltpu.VMEM((2, 3, rows // 16 + 2, 8, LANES), jnp.float32)],
        compiler_params=pltpu.CompilerParams(vmem_limit_bytes=VMEM_BYTES),
        name="relax",
    )(*fixed, from_left, from_right, from_prev, from_next, field, sigma, current)


def moved(value, axis, steps):
    count = lax.axis_size(axis)
    return lax.ppermute(value, axis, [(i, (i + steps) % count) for i in range(count)])


def local(field, sigma, current, rotor_cycle, skew_list):
    rotor = [rotor_cycle] + [moved(rotor_cycle, "az", s) for s in range(2, lax.axis_size("az") - 1)]
    to_left, to_right = pack_cols(field, sigma, current, rotor_cycle)
    from_left, from_right = moved(to_right, "az", 1), moved(to_left, "az", -1)
    to_prev, to_next = pack_rows(field, sigma, current, to_left)
    from_prev, from_next = moved(to_next, "ta", 1), moved(to_prev, "ta", -1)
    small_to_prev, small_to_next = place_edges(rotor, skew_list, from_left, from_right)
    small_prev, small_next = moved(small_to_next, "ta", 1), moved(small_to_prev, "ta", -1)
    placed = place_cycle(rotor, skew_list, from_left, from_right, small_to_prev)
    return relax(
        placed, small_prev, small_next, from_left, from_right, from_prev, from_next, field, sigma, current
    )


def solution(mesh):
    placed = (P(None, "ta", "az"), P(None, "ta", "az"), P(None, "ta", "az"), P("ta", "az"), P("ta"))
    return jax.shard_map(
        local, mesh=mesh, in_specs=placed, out_specs=P(None, "ta", "az"), check_vma=False
    )
```

```python
import functools

import jax
import jax.numpy as jnp
from jax import lax
from jax.experimental import pallas as pl
from jax.experimental.pallas import tpu as pltpu
from jax.sharding import PartitionSpec as P

LANES = 128
EDGE = 8
LAG = 4
VMEM_BYTES = 60 * 1024 * 1024


def checker(rows):
    sub = lax.broadcasted_iota(jnp.int32, (rows, LANES), 0)
    lane = lax.broadcasted_iota(jnp.int32, (rows, LANES), 1)
    return ((sub + lane) & 1) == 0


def f32(value):
    return value.astype(jnp.float32)


def split_high_low(value):
    high = f32(value.astype(jnp.bfloat16))
    return high, value - high


def rows_kernel(u_top, u_bot, s_top, s_bot, j_top, j_bot, after, to_prev, to_next, *, pairs, tiles):
    even8 = checker(8)
    sub = lax.broadcasted_iota(jnp.int32, (8, LANES), 0)
    field_rows = sub < 5

    def pair_rows(m, _):
        for c in range(tiles):
            cols = slice(c * LANES, (c + 1) * LANES)
            for u_ref, s_ref, j_ref, half, out_ref in (
                (u_top, s_top, j_top, 0, to_prev),
                (u_bot, s_bot, j_bot, 8, to_next),
            ):
                eo = []
                for ref in (u_ref, s_ref, j_ref):
                    first = f32(ref[2 * m, :, cols])
                    second = f32(ref[2 * m + 1, :, cols])
                    if first.shape[0] == 16:
                        first = first[half : half + 8]
                        second = second[half : half + 8]
                    eo.append((first, second))
                for colour in (0, 1):
                    pick = [
                        jnp.where(even8, a, b) if colour == 0 else jnp.where(even8, b, a)
                        for a, b in eo
                    ]
                    high, low = split_high_low(pick[0])
                    sig, cur = pick[1], pick[2]
                    if half == 0:
                        sig = pltpu.roll(sig, 5, 0)
                        cur = pltpu.roll(cur, 5, 0)
                    else:
                        high = pltpu.roll(high, 5, 0)
                        low = pltpu.roll(low, 5, 0)
                    both = jnp.concatenate(
                        [jnp.where(field_rows, high, sig), jnp.where(field_rows, low, cur)], 0
                    )
                    out_ref[colour, m, :, cols] = both.astype(jnp.bfloat16)
        return 0

    lax.fori_loop(0, pairs, pair_rows, 0)


def cols_kernel(
    u_left, u_right, s_left, s_right, j_left, j_right, to_left, to_right, *, pairs, blocks
):
    even16 = checker(16)
    slot = lax.broadcasted_iota(jnp.int32, (8, LANES), 1) // 4
    slots = LANES // 4
    for q in range(blocks):
        rows = slice(16 * q, 16 * q + 16)
        for refs, out_ref, near_at, far_at in (
            ((u_left, s_left, j_left), to_left, 1, 2),
            ((u_right, s_right, j_right), to_right, 0, 1),
        ):
            packed = []
            for ref in refs:
                total = jnp.zeros((8, LANES), jnp.float32)
                for m in range(pairs):
                    first = f32(ref[2 * m, rows, :])
                    second = f32(ref[2 * m + 1, rows, :])
                    red = jnp.where(even16, first, second)
                    black = jnp.where(even16, second, first)
                    for w in (0, 1):
                        g = m + pairs * w
                        near = pltpu.roll(red[8 * w : 8 * w + 8], (8 * g + 4) % LANES, 1)
                        far = pltpu.roll(black[8 * w : 8 * w + 8], (8 * g + 8) % LANES, 1)
                        total = jnp.where(slot == (2 * g + near_at) % slots, near, total)
                        total = jnp.where(slot == (2 * g + far_at) % slots, far, total)
                packed.append(total)
            high, low = split_high_low(packed[0])
            out_ref[q, 0] = jnp.concatenate([high, low], 0).astype(jnp.bfloat16)
            out_ref[q, 1] = jnp.concatenate([packed[1], packed[2]], 0).astype(jnp.bfloat16)


def whole_at(shape, index):
    return pl.BlockSpec(shape, lambda i: index)


def pack_rows(field, sigma, current, after):
    layers, rows, cols = field.shape
    pairs, tiles = layers // 2, cols // LANES

    def row_specs(height):
        shape = (layers, height, cols)
        return [whole_at(shape, (0, 0, 0)), whole_at(shape, (0, rows // height - 1, 0))]

    shape = (2, pairs, 16, cols)
    return pl.pallas_call(
        functools.partial(rows_kernel, pairs=pairs, tiles=tiles),
        grid=(1,),
        in_specs=row_specs(8) + row_specs(16) * 2 + [pl.BlockSpec(memory_space=pl.ANY)],
        out_specs=[whole_at(shape, (0,) * 4)] * 2,
        out_shape=[jax.ShapeDtypeStruct(shape, jnp.bfloat16)] * 2,
        compiler_params=pltpu.CompilerParams(vmem_limit_bytes=VMEM_BYTES),
        cost_estimate=pl.CostEstimate(flops=0, bytes_accessed=12 << 20, transcendentals=0),
        name="pack_rows",
    )(field, field, sigma, sigma, current, current, after)


def pack_cols(field, sigma, current):
    layers, rows, cols = field.shape
    pairs, tiles, blocks = layers // 2, cols // LANES, rows // 16
    part = 2
    shape = (layers, 16 * part, LANES)
    col_specs = [pl.BlockSpec(shape, lambda i: (0, i, 0)), pl.BlockSpec(shape, lambda i: (0, i, tiles - 1))]
    out_spec = pl.BlockSpec((part, 2, 16, LANES), lambda i: (i, 0, 0, 0))
    return pl.pallas_call(
        functools.partial(cols_kernel, pairs=pairs, blocks=part),
        grid=(blocks // part,),
        in_specs=col_specs * 3,
        out_specs=[out_spec] * 2,
        out_shape=[jax.ShapeDtypeStruct((blocks, 2, 16, LANES), jnp.bfloat16)] * 2,
        compiler_params=pltpu.CompilerParams(vmem_limit_bytes=VMEM_BYTES),
        cost_estimate=pl.CostEstimate(flops=0, bytes_accessed=16 << 20, transcendentals=0),
        name="pack_cols",
    )(field, field, sigma, sigma, current, current)


def small_kernel(skew, r_top, r_bot, l_near, l_far, e_near, e_far, small_prev, small_next, *, rows, tiles):
    sub = lax.broadcasted_iota(jnp.int32, (16, LANES), 0)
    for out_ref, r_ref, left, right, first in (
        (small_prev, r_top, l_near, e_near, 0),
        (small_next, r_bot, l_far, e_far, rows - 16),
    ):
        for i in (0, 1):
            out_ref[i] = left[0, i]
            out_ref[2 + i] = right[0, i]
        for c in range(tiles):
            out_ref[4 + c] = r_ref[:, c * LANES : (c + 1) * LANES]
        out_ref[4 + tiles] = f32(turns(skew, first, sub)).astype(jnp.bfloat16)


def turns(skew, row, sub):
    turn = jnp.zeros(sub.shape, jnp.int32)
    for i in range(16):
        turn = jnp.where(sub == i, skew[row + i], turn)
    return turn


def pack_small(rotor_cycle, skew_list, from_left, from_right):
    rows, cols = rotor_cycle.shape
    tiles, blocks = cols // LANES, rows // 16
    ends = (0, blocks - 1)
    side = [whole_at((1, 2, 16, LANES), (i, 0, 0, 0)) for i in ends]
    out = (tiles + 5, 16, LANES)
    return pl.pallas_call(
        functools.partial(small_kernel, rows=rows, tiles=tiles),
        grid=(1,),
        in_specs=[pl.BlockSpec(memory_space=pltpu.SMEM)] + [whole_at((16, cols), (i, 0)) for i in ends] + side * 2,
        out_specs=[whole_at(out, (0,) * 3)] * 2,
        out_shape=[jax.ShapeDtypeStruct(out, jnp.bfloat16)] * 2,
        compiler_params=pltpu.CompilerParams(vmem_limit_bytes=VMEM_BYTES),
        name="pack_small",
    )(skew_list, rotor_cycle, rotor_cycle, from_left, from_left, from_right, from_right)


def rotor_kernel(rotor, small_prev, small_next, out_ref, *, blocks, tiles):
    for c in range(tiles):
        for b in range(blocks):
            out_ref[b, c] = rotor[16 * b : 16 * b + 16, c * LANES : (c + 1) * LANES]
        out_ref[blocks, c] = small_prev[4 + c]
        out_ref[blocks + 1, c] = small_next[4 + c]


def pack_rotor(rotor_cycle, small_prev, small_next):
    rows, cols = rotor_cycle.shape
    tiles, blocks = cols // LANES, rows // 16
    small = whole_at((tiles + 5, 16, LANES), (0, 0, 0))
    out = (blocks + 2, tiles, 16, LANES)
    return pl.pallas_call(
        functools.partial(rotor_kernel, blocks=blocks, tiles=tiles),
        grid=(1,),
        in_specs=[whole_at((rows, cols), (0, 0)), small, small],
        out_specs=whole_at(out, (0,) * 4),
        out_shape=jax.ShapeDtypeStruct(out, jnp.bfloat16),
        compiler_params=pltpu.CompilerParams(vmem_limit_bytes=VMEM_BYTES),
        name="pack_rotor",
    )(rotor_cycle, small_prev, small_next)


def place_block(turn, rotor, b, slots, tiles):
    lane16 = lax.broadcasted_iota(jnp.int32, (16, LANES), 1)
    panels = slots * tiles
    bits = (panels - 1).bit_length()
    want = [(panels - tiles - 1 + p) % panels for p in range(tiles + 2)]
    needs = [set(want)]
    for bit in range(bits):
        needs.append(needs[-1] | {(q - (1 << bit)) % panels for q in needs[-1]})
    cur = {q: f32(rotor[slots - 1 - q // tiles][b, q % tiles]) for q in sorted(needs[bits])}
    for bit in reversed(range(bits)):
        on = ((turn >> bit) & 1) == 1
        cur = {q: jnp.where(on, cur[(q - (1 << bit)) % panels], cur[q]) for q in sorted(needs[bit])}
    placed = [cur[want[p + 1]] for p in range(tiles)]
    return placed + [jnp.where(lane16 < LANES // 2, cur[want[tiles + 1]], cur[want[0]])]


def make_steps(ins, out_ref, scratch, pairs, rows, tiles):
    small_prev, small_next, from_left, from_right, from_prev, from_next, u_ref, s_ref, j_ref = ins
    red_a, red_b, black_a, black_b, sig_r, sig_b, cur_r, cur_b, side = scratch
    blocks = rows // 16
    even8 = checker(8)
    even16 = checker(16)
    lane = lax.broadcasted_iota(jnp.int32, (8, LANES), 1)
    lane_first = lane == 0
    lane_last = lane == LANES - 1
    left_slot = (lane & 7) < 4

    def decode(q, left, right):
        left0, left1, right0, right1 = f32(left[0]), f32(left[1]), f32(right[0]), f32(right[1])
        items = (
            (left0[:8] + left0[8:], right0[:8] + right0[8:], 1.0),
            (left1[:8], right1[:8], 1.0 / 48.0),
            (left1[8:], right1[8:], 0.25),
        )
        for item, (a, b, scale) in enumerate(items):
            side[0, item, q] = jnp.where(left_slot, a, b) * scale
            side[1, item, q] = jnp.where(left_slot, b, a) * scale

    def start():
        for q in range(blocks):
            decode(q, from_left[q], from_right[q])
        decode(blocks, small_prev[0:2], small_prev[2:4])
        decode(blocks + 1, small_next[0:2], small_next[2:4])

    def load(m, with_field):
        fields = ((red_a, sig_r, cur_r), (black_a, sig_b, cur_b))
        for colour in (0, 1):
            u_dst, s_dst, j_dst = fields[colour]
            for c in range(tiles):
                cols = slice(c * LANES, (c + 1) * LANES)
                both = f32(from_prev[colour, 0, :, cols])
                if with_field:
                    u_dst[m + 1, c, pl.ds(EDGE - 5, 8), :] = both[:8] + both[8:]
                s_dst[m, c, pl.ds(0, 8), :] = both[:8] * (1.0 / 48.0)
                j_dst[m, c, pl.ds(0, 8), :] = both[8:] * 0.25
                both = f32(from_next[colour, 0, :, cols])
                if with_field:
                    u_dst[m + 1, c, pl.ds(EDGE + rows, 8), :] = both[:8] + both[8:]
                s_dst[m, c, pl.ds(EDGE + rows - 5, 8), :] = both[:8] * (1.0 / 48.0)
                j_dst[m, c, pl.ds(EDGE + rows - 5, 8), :] = both[8:] * 0.25

        def own_rows(q, _):
            at = pl.ds(pl.multiple_of(16 * q, 16), 16)
            to = pl.ds(pl.multiple_of(16 * q + EDGE, 8), 16)
            for c in range(tiles):
                cols = slice(c * LANES, (c + 1) * LANES)
                if with_field:
                    a, b = u_ref[0, at, cols], u_ref[1, at, cols]
                    red_a[m + 1, c, to, :] = jnp.where(even16, a, b)
                    black_a[m + 1, c, to, :] = jnp.where(even16, b, a)
                a, b = f32(s_ref[0, at, cols]) * (1.0 / 48.0), f32(s_ref[1, at, cols]) * (1.0 / 48.0)
                sig_r[m, c, to, :] = jnp.where(even16, a, b)
                sig_b[m, c, to, :] = jnp.where(even16, b, a)
                a, b = f32(j_ref[0, at, cols]) * 0.25, f32(j_ref[1, at, cols]) * 0.25
                cur_r[m, c, to, :] = jnp.where(even16, a, b)
                cur_b[m, c, to, :] = jnp.where(even16, b, a)
            return 0

        lax.fori_loop(0, blocks, own_rows, 0)

        for colour in (0, 1):
            u_dst, s_dst, j_dst = fields[colour]
            for item, (dst, plane) in enumerate(((u_dst, m + 1), (s_dst, m), (j_dst, m))):
                if item == 0 and not with_field:
                    continue
                for w in (0, 1):
                    turn = lax.rem(2 * LANES + 124 - 4 * colour - 8 * (m + pairs * w), LANES)
                    for q in range(blocks):
                        dst[plane, tiles, pl.ds(EDGE + 16 * q + 8 * w, 8), :] = pltpu.roll(side[colour, item, q], turn, 1)
                    if w == 1:
                        dst[plane, tiles, pl.ds(0, 8), :] = pltpu.roll(side[colour, item, blocks], turn, 1)
                    else:
                        dst[plane, tiles, pl.ds(EDGE + rows, 8), :] = pltpu.roll(side[colour, item, blocks + 1], turn, 1)

    def half_step(m, colour, own, other, sig, cur, start, count, outputs, write):
        def row_tile(at):
            centre = [other[m + 1, c, pl.ds(at, 8), :] for c in range(tiles + 1)]
            ahead = [pltpu.roll(x, 1, 1) for x in centre]
            back = [pltpu.roll(x, LANES - 1, 1) for x in centre]
            for c in range(outputs):
                left = jnp.where(lane_first, ahead[c - 1], ahead[c])
                right = jnp.where(lane_last, back[(c + 1) % (tiles + 1)], back[c])
                below = other[m, c, pl.ds(at, 8), :]
                above = other[m + 2, c, pl.ds(at, 8), :]
                outer = jnp.where(even8, below, above) if colour == 0 else jnp.where(even8, above, below)
                near = other[m + 1, c, pl.ds(at + 1, 8), :] - other[m + 1, c, pl.ds(at - 1, 8), :]
                far = own[m + 1, c, pl.ds(at + 2, 8), :] - own[m + 1, c, pl.ds(at - 2, 8), :]
                total = (left + right) + (centre[c] + outer)
                new = cur[m, c, pl.ds(at, 8), :] + 0.25 * total - sig[m, c, pl.ds(at, 8), :] * (8.0 * near - far)
                write(m, c, at, new)

        for r in range(count):
            row_tile(start + 8 * r)

    def keep(buf):
        def write(m, c, at, new):
            buf[m + 1, c, pl.ds(at, 8), :] = new

        return write

    def emit(m, c, at, new):
        red = red_a[m + 1, c, pl.ds(at, 8), :]
        cols = slice(c * LANES, (c + 1) * LANES)
        to = pl.ds(pl.multiple_of(at - EDGE, 8), 8)
        out_ref[0, to, cols] = jnp.where(even8, red, new)
        out_ref[1, to, cols] = jnp.where(even8, new, red)

    wide = (EDGE - 4, rows // 8 + 1, tiles + 1)
    last = (EDGE, rows // 8, tiles)

    def step(number, m):
        own, other, sig, cur, where, write = (
            (red_a, black_a, sig_r, cur_r, wide, keep(red_b)),
            (black_a, red_b, sig_b, cur_b, wide, keep(black_b)),
            (red_b, black_b, sig_r, cur_r, wide, keep(red_a)),
            (black_b, red_a, sig_b, cur_b, last, emit),
        )[number - 1]
        half_step(m, (number - 1) % 2, own, other, sig, cur, *where, write)

    return start, load, step


def upper_kernel(*refs, pairs, rows, tiles):
    ins, out_ref, saved, scratch, sem = refs[:9], refs[9], refs[10:13], refs[13:22], refs[22]
    g = pl.program_id(0)
    start, load, step = make_steps(ins, out_ref, scratch, pairs, rows, tiles)
    red_a, red_b, black_a, black_b = scratch[:4]
    copies = [
        pltpu.make_async_copy(buf.at[pl.ds(first, 2)], to, sem.at[i])
        for i, (buf, first, to) in enumerate(zip((red_b, black_b, red_a), (2, 3, 4), saved))
    ]

    @pl.when(g == 0)
    def first():
        start()
        zero = jnp.zeros((8, LANES), jnp.float32)
        for buf in (red_a, red_b, black_a, black_b):
            for c in range(tiles + 1):
                for r in range(rows // 8 + 2):
                    buf[pairs + 1, c, pl.ds(8 * r, 8), :] = zero

    load(pairs - 1 - g, True)
    for number in (1, 2, 3, 4):

        @pl.when(g >= number)
        def run(number=number):
            step(number, pairs - 1 - g + number)

        if number < 4:

            @pl.when(g == pairs - 1)
            def save(number=number):
                copies[number - 1].start()

    @pl.when(g == pairs - 1)
    def finish():
        for copy in copies:
            copy.wait()


def lower_kernel(*refs, slots, pairs, rows, tiles):
    saved, skew, rotor, refs = refs[1:4], refs[4], refs[5 : 5 + slots], refs[5 + slots :]
    ins, out_ref, scratch, sem = refs[:9], refs[9], refs[10:19], refs[19]
    small_prev, small_next = ins[:2]
    g = pl.program_id(0)
    blocks = rows // 16
    start, load, step = make_steps(ins, out_ref, scratch, pairs, rows, tiles)
    red_a, red_b, black_a, black_b = scratch[:4]
    copies = [
        pltpu.make_async_copy(of, buf.at[pl.ds(first, 2)], sem.at[i])
        for i, (buf, first, of) in enumerate(zip((red_b, black_b, red_a), (2, 3, 4), saved))
    ]

    @pl.when(g == 0)
    def first():
        for copy in copies:
            copy.start()
        start()
        sub16 = lax.broadcasted_iota(jnp.int32, (16, LANES), 0)

        def fill(values, spots):
            for c, value in enumerate(values):
                for buf in (red_a, red_b, black_a, black_b):
                    for half, to in spots:
                        buf[0, c, to, :] = value[8 * half : 8 * half + 8]

        def placed_rows(b, _):
            spots = [(half, pl.ds(pl.multiple_of(16 * b + EDGE + 8 * half, 8), 8)) for half in (0, 1)]
            fill(place_block(turns(skew, 16 * b, sub16), rotor, b, slots, tiles), spots)
            return 0

        lax.fori_loop(0, blocks, placed_rows, 0)
        for i, (small, spot) in enumerate(((small_prev, (1, pl.ds(0, 8))), (small_next, (0, pl.ds(EDGE + rows, 8))))):
            turn = f32(small[4 + tiles]).astype(jnp.int32)
            fill(place_block(turn, rotor, blocks + i, slots, tiles), [spot])

    @pl.when(g < 2)
    def load_all():
        load(g, True)

    @pl.when((g >= 2) & (g < LAG))
    def load_coefficients():
        load(g, False)

    def several(number, count):
        def body(i, _):
            step(number, count - 1 - i)
            return 0

        lax.fori_loop(0, count, body, 0)

    @pl.when(g == 1)
    def early():
        for copy in copies:
            copy.wait()
        several(1, 1)
        several(2, 2)

    @pl.when(g == 2)
    def middle():
        several(3, 3)

    @pl.when(g >= 3)
    def late():
        step(4, 6 - g)


def relax(rotor, skew_list, small_prev, small_next, from_left, from_right, from_prev, from_next, field, sigma, current):
    layers, rows, cols = field.shape
    pairs, tiles, slots = layers // 2, cols // LANES, len(rotor)
    plane = (tiles + 1, rows + 2 * EDGE, LANES)
    anywhere = pl.BlockSpec(memory_space=pl.ANY)

    def whole(array):
        zeros = (0,) * array.ndim
        return pl.BlockSpec(array.shape, lambda g: zeros)

    def specs(field_at, rest_at):
        halo = pl.BlockSpec((2, 1, 16, cols), lambda g: (0, rest_at(g), 0, 0))
        rest = pl.BlockSpec((2, rows, cols), lambda g: (rest_at(g), 0, 0))
        mine = pl.BlockSpec((2, rows, cols), lambda g: (field_at(g), 0, 0))
        return [whole(a) for a in ins[:4]] + [halo, halo, mine, rest, rest]

    def scratch(states, coefs):
        return (
            [pltpu.VMEM((states, *plane), jnp.float32)] * 4
            + [pltpu.VMEM((coefs, *plane), jnp.float32)] * 4
            + [pltpu.VMEM((2, 3, rows // 16 + 2, 8, LANES), jnp.float32), pltpu.SemaphoreType.DMA((3,))]
        )

    ins = [small_prev, small_next, from_left, from_right, from_prev, from_next, field, sigma, current]
    params = pltpu.CompilerParams(vmem_limit_bytes=VMEM_BYTES)
    result = jax.ShapeDtypeStruct(field.shape, jnp.float32)
    kept = jax.ShapeDtypeStruct((2, *plane), jnp.float32)
    cost = pl.CostEstimate(flops=0, bytes_accessed=64 << 20, transcendentals=0)

    def down(g):
        return pairs - 1 - g

    out, *saved = pl.pallas_call(
        functools.partial(upper_kernel, pairs=pairs, rows=rows, tiles=tiles),
        grid=(pairs,),
        in_specs=specs(down, down),
        out_specs=[pl.BlockSpec((2, rows, cols), lambda g: (jnp.minimum(pairs - 1, pairs + LAG - 1 - g), 0, 0))]
        + [anywhere] * 3,
        out_shape=[result, kept, kept, kept],
        scratch_shapes=scratch(pairs + 2, pairs),
        compiler_params=params,
        cost_estimate=cost,
        name="upper",
    )(*ins)
    return pl.pallas_call(
        functools.partial(lower_kernel, slots=slots, pairs=pairs, rows=rows, tiles=tiles),
        grid=(2 * LAG - 1,),
        in_specs=[anywhere] * 4
        + [pl.BlockSpec(memory_space=pltpu.SMEM)]
        + [whole(a) for a in rotor]
        + specs(lambda g: jnp.minimum(g, 1), lambda g: jnp.minimum(g, LAG - 1)),
        out_specs=pl.BlockSpec((2, rows, cols), lambda g: (jnp.minimum(LAG - 1, 2 * LAG - 2 - g), 0, 0)),
        out_shape=result,
        scratch_shapes=scratch(LAG + 2, LAG),
        input_output_aliases={0: 0},
        compiler_params=params,
        name="lower",
    )(out, *saved, skew_list, *rotor, *ins)


def moved(value, axis, steps):
    count = lax.axis_size(axis)
    return lax.ppermute(value, axis, [(i, (i + steps) % count) for i in range(count)])


def local(field, sigma, current, rotor_cycle, skew_list):
    to_left, to_right = pack_cols(field, sigma, current)
    from_left, from_right = moved(to_right, "az", 1), moved(to_left, "az", -1)
    to_prev, to_next = pack_rows(field, sigma, current, to_left)
    from_prev, from_next = moved(to_next, "ta", 1), moved(to_prev, "ta", -1)
    small_to_prev, small_to_next = pack_small(rotor_cycle, skew_list, from_left, from_right)
    small_prev, small_next = moved(small_to_next, "ta", 1), moved(small_to_prev, "ta", -1)
    rotor = pack_rotor(rotor_cycle, small_prev, small_next)
    rotor = [rotor] + [moved(rotor, "az", s) for s in range(1, lax.axis_size("az"))]
    return relax(
        rotor, skew_list, small_prev, small_next, from_left, from_right, from_prev, from_next, field, sigma, current
    )


def solution(mesh):
    placed = (P(None, "ta", "az"), P(None, "ta", "az"), P(None, "ta", "az"), P("ta", "az"), P("ta"))
    return jax.shard_map(
        local, mesh=mesh, in_specs=placed, out_specs=P(None, "ta", "az"), check_vma=False
    )
```

```python
import functools

import jax
import jax.numpy as jnp
from jax import lax
from jax.experimental import pallas as pl
from jax.experimental.pallas import tpu as pltpu
from jax.sharding import PartitionSpec as P

LANES = 128
EDGE = 8
LAG = 4
DEPTH = 4
VMEM_BYTES = 60 * 1024 * 1024


def checker(rows):
    sub = lax.broadcasted_iota(jnp.int32, (rows, LANES), 0)
    lane = lax.broadcasted_iota(jnp.int32, (rows, LANES), 1)
    return ((sub + lane) & 1) == 0


def f32(value):
    return value.astype(jnp.float32)


def split_high_low(value):
    high = f32(value.astype(jnp.bfloat16))
    return high, value - high


def rows_kernel(u_top, u_bot, s_top, s_bot, j_top, j_bot, after, to_prev, to_next, *, pairs, tiles):
    even8 = checker(8)
    sub = lax.broadcasted_iota(jnp.int32, (8, LANES), 0)
    field_rows = sub < 5

    def pair_rows(m, _):
        for c in range(tiles):
            cols = slice(c * LANES, (c + 1) * LANES)
            for u_ref, s_ref, j_ref, half, out_ref in (
                (u_top, s_top, j_top, 0, to_prev),
                (u_bot, s_bot, j_bot, 8, to_next),
            ):
                eo = []
                for ref in (u_ref, s_ref, j_ref):
                    first = f32(ref[2 * m, :, cols])
                    second = f32(ref[2 * m + 1, :, cols])
                    if first.shape[0] == 16:
                        first = first[half : half + 8]
                        second = second[half : half + 8]
                    eo.append((first, second))
                for colour in (0, 1):
                    pick = [
                        jnp.where(even8, a, b) if colour == 0 else jnp.where(even8, b, a)
                        for a, b in eo
                    ]
                    high, low = split_high_low(pick[0])
                    sig, cur = pick[1], pick[2]
                    if half == 0:
                        sig = pltpu.roll(sig, 5, 0)
                        cur = pltpu.roll(cur, 5, 0)
                    else:
                        high = pltpu.roll(high, 5, 0)
                        low = pltpu.roll(low, 5, 0)
                    both = jnp.concatenate(
                        [jnp.where(field_rows, high, sig), jnp.where(field_rows, low, cur)], 0
                    )
                    out_ref[colour, m, :, cols] = both.astype(jnp.bfloat16)
        return 0

    lax.fori_loop(0, pairs, pair_rows, 0)


def cols_kernel(
    u_left, u_right, s_left, s_right, j_left, j_right, rotor, to_left, to_right, *, pairs, tiles, blocks
):
    even16 = checker(16)
    slot = lax.broadcasted_iota(jnp.int32, (8, LANES), 1) // 4
    slots = LANES // 4
    for q in range(blocks):
        rows = slice(16 * q, 16 * q + 16)
        for c in range(tiles):
            panel = rotor[rows, c * LANES : (c + 1) * LANES]
            to_left[q, 2 + c] = panel
            to_right[q, 2 + c] = panel
        for refs, out_ref, near_at, far_at in (
            ((u_left, s_left, j_left), to_left, 1, 2),
            ((u_right, s_right, j_right), to_right, 0, 1),
        ):
            packed = []
            for ref in refs:
                total = jnp.zeros((8, LANES), jnp.float32)
                for m in range(pairs):
                    first = f32(ref[2 * m, rows, :])
                    second = f32(ref[2 * m + 1, rows, :])
                    red = jnp.where(even16, first, second)
                    black = jnp.where(even16, second, first)
                    for w in (0, 1):
                        g = m + pairs * w
                        near = pltpu.roll(red[8 * w : 8 * w + 8], (8 * g + 4) % LANES, 1)
                        far = pltpu.roll(black[8 * w : 8 * w + 8], (8 * g + 8) % LANES, 1)
                        total = jnp.where(slot == (2 * g + near_at) % slots, near, total)
                        total = jnp.where(slot == (2 * g + far_at) % slots, far, total)
                packed.append(total)
            high, low = split_high_low(packed[0])
            out_ref[q, 0] = jnp.concatenate([high, low], 0).astype(jnp.bfloat16)
            out_ref[q, 1] = jnp.concatenate([packed[1], packed[2]], 0).astype(jnp.bfloat16)


def whole_at(shape, index):
    return pl.BlockSpec(shape, lambda i: index)


def pack_rows(field, sigma, current, after):
    layers, rows, cols = field.shape
    pairs, tiles = layers // 2, cols // LANES

    def row_specs(height):
        shape = (layers, height, cols)
        return [whole_at(shape, (0, 0, 0)), whole_at(shape, (0, rows // height - 1, 0))]

    shape = (2, pairs, 16, cols)
    return pl.pallas_call(
        functools.partial(rows_kernel, pairs=pairs, tiles=tiles),
        grid=(1,),
        in_specs=row_specs(8) + row_specs(16) * 2 + [pl.BlockSpec(memory_space=pl.ANY)],
        out_specs=[whole_at(shape, (0,) * 4)] * 2,
        out_shape=[jax.ShapeDtypeStruct(shape, jnp.bfloat16)] * 2,
        compiler_params=pltpu.CompilerParams(vmem_limit_bytes=VMEM_BYTES),
        cost_estimate=pl.CostEstimate(flops=0, bytes_accessed=12 << 20, transcendentals=0),
        name="pack_rows",
    )(field, field, sigma, sigma, current, current, after)


def pack_cols(field, sigma, current, rotor_cycle):
    layers, rows, cols = field.shape
    pairs, tiles, blocks = layers // 2, cols // LANES, rows // 16
    part = 2
    shape = (layers, 16 * part, LANES)
    col_specs = [pl.BlockSpec(shape, lambda i: (0, i, 0)), pl.BlockSpec(shape, lambda i: (0, i, tiles - 1))]
    out_spec = pl.BlockSpec((part, tiles + 2, 16, LANES), lambda i: (i, 0, 0, 0))
    return pl.pallas_call(
        functools.partial(cols_kernel, pairs=pairs, tiles=tiles, blocks=part),
        grid=(blocks // part,),
        in_specs=col_specs * 3 + [pl.BlockSpec((16 * part, cols), lambda i: (i, 0))],
        out_specs=[out_spec] * 2,
        out_shape=[jax.ShapeDtypeStruct((blocks, tiles + 2, 16, LANES), jnp.bfloat16)] * 2,
        compiler_params=pltpu.CompilerParams(vmem_limit_bytes=VMEM_BYTES),
        cost_estimate=pl.CostEstimate(flops=0, bytes_accessed=16 << 20, transcendentals=0),
        name="pack_cols",
    )(field, field, sigma, sigma, current, current, rotor_cycle)


def place_block(row, skew, rotor, from_left, from_right, at, slots, tiles):
    lane16 = lax.broadcasted_iota(jnp.int32, (16, LANES), 1)
    sub16 = lax.broadcasted_iota(jnp.int32, (16, LANES), 0)
    panels = slots * tiles
    bits = (panels - 1).bit_length()
    want = [(panels - tiles - 1 + p) % panels for p in range(tiles + 2)]
    needs = [set(want)]
    for bit in range(bits):
        needs.append(needs[-1] | {(q - (1 << bit)) % panels for q in needs[-1]})
    turn = jnp.zeros((16, LANES), jnp.int32)
    for i in range(16):
        turn = jnp.where(sub16 == i, skew[row + i], turn)

    def panel(steps, c):
        if steps in (1, slots - 1):
            return (from_left if steps == 1 else from_right)[at, 2 + c]
        source = rotor[0] if steps == 0 else rotor[steps - 1]
        return source[pl.ds(pl.multiple_of(16 * at, 16), 16), c * LANES : (c + 1) * LANES]

    cur = {q: f32(panel(slots - 1 - q // tiles, q % tiles)) for q in sorted(needs[bits])}
    for bit in reversed(range(bits)):
        on = ((turn >> bit) & 1) == 1
        cur = {q: jnp.where(on, cur[(q - (1 << bit)) % panels], cur[q]) for q in sorted(needs[bit])}
    placed = [cur[want[p + 1]] for p in range(tiles)]
    placed.append(jnp.where(lane16 < LANES // 2, cur[want[tiles + 1]], cur[want[0]]))
    return [x.astype(jnp.bfloat16) for x in placed]


def place_edges_kernel(skew, *refs, slots, rows, tiles):
    near, far, outs = refs[:slots], refs[slots : 2 * slots], refs[2 * slots :]
    for out_ref, ins, row in ((outs[0], near, 0), (outs[1], far, rows - 16)):
        from_left, from_right = ins[slots - 2 :]
        for i in (0, 1):
            out_ref[i] = from_left[0, i]
            out_ref[2 + i] = from_right[0, i]
        for c, value in enumerate(place_block(row, skew, ins[: slots - 2], from_left, from_right, 0, slots, tiles)):
            out_ref[4 + c] = value


def place_edges(rotor, skew_list, from_left, from_right):
    rows, cols = rotor[0].shape
    tiles, slots, blocks = cols // LANES, len(rotor) + 2, rows // 16

    def specs(i):
        side = whole_at((1, tiles + 2, 16, LANES), (i, 0, 0, 0))
        return [whole_at((16, cols), (i, 0))] * len(rotor) + [side, side]

    out = (tiles + 5, 16, LANES)
    ins = [*rotor, from_left, from_right]
    return pl.pallas_call(
        functools.partial(place_edges_kernel, slots=slots, rows=rows, tiles=tiles),
        grid=(1,),
        in_specs=[pl.BlockSpec(memory_space=pltpu.SMEM)] + specs(0) + specs(blocks - 1),
        out_specs=[whole_at(out, (0,) * 3)] * 2,
        out_shape=[jax.ShapeDtypeStruct(out, jnp.bfloat16)] * 2,
        compiler_params=pltpu.CompilerParams(vmem_limit_bytes=VMEM_BYTES),
        cost_estimate=pl.CostEstimate(flops=0, bytes_accessed=1 << 20, transcendentals=0),
        name="place_edges",
    )(skew_list, *ins, *ins)


def place_kernel(skew, *refs, slots, rows, tiles):
    rotor = refs[: slots - 2]
    from_left, from_right, after, placed_ref = refs[slots - 2 :]

    def rotor_rows(b, _):
        at = pl.ds(pl.multiple_of(16 * b, 16), 16)
        for p, value in enumerate(place_block(16 * b, skew, rotor, from_left, from_right, b, slots, tiles)):
            placed_ref[p, at, :] = value
        return 0

    lax.fori_loop(0, rows // 16, rotor_rows, 0)


def place_cycle(rotor, skew_list, from_left, from_right, after):
    rows, cols = rotor[0].shape
    tiles = cols // LANES
    sides = whole_at(from_left.shape, (0, 0, 0, 0))
    out = (tiles + 1, rows, LANES)
    return pl.pallas_call(
        functools.partial(place_kernel, slots=len(rotor) + 2, rows=rows, tiles=tiles),
        grid=(1,),
        in_specs=[pl.BlockSpec(memory_space=pltpu.SMEM)]
        + [whole_at((rows, cols), (0, 0))] * len(rotor)
        + [sides, sides, pl.BlockSpec(memory_space=pl.ANY)],
        out_specs=whole_at(out, (0,) * 3),
        out_shape=jax.ShapeDtypeStruct(out, jnp.bfloat16),
        compiler_params=pltpu.CompilerParams(vmem_limit_bytes=VMEM_BYTES),
        cost_estimate=pl.CostEstimate(flops=0, bytes_accessed=4 << 20, transcendentals=0),
        name="place_cycle",
    )(skew_list, *rotor, from_left, from_right, after)


def relax_kernel(placed, small_prev, small_next, from_left, from_right, from_prev, from_next,
     u_ref, s_ref, j_ref, out_ref,
     red_a, red_b, black_a, black_b, sig_r, sig_b, cur_r, cur_b, side, u_buf, s_buf, j_buf, sem, *, pairs, rows, tiles):
    g = pl.program_id(0)
    blocks = rows // 16
    even8 = checker(8)
    even16 = checker(16)
    lane = lax.broadcasted_iota(jnp.int32, (8, LANES), 1)
    lane_first = lane == 0
    lane_last = lane == LANES - 1

    def fetch(m):
        slot = lax.rem(m, DEPTH)
        return [
            pltpu.make_async_copy(ref.at[2 * m + half], buf.at[slot, half], sem.at[slot, i, half])
            for i, (ref, buf) in enumerate(((u_ref, u_buf), (s_ref, s_buf), (j_ref, j_buf)))
            for half in (0, 1)
        ]

    @pl.when(g == 0)
    def prologue():
        for m in range(min(DEPTH, pairs)):
            for copy in fetch(m):
                copy.start()

        def fill(value, c, spots):
            zero = jnp.zeros((8, LANES), jnp.float32)
            for buf in (red_a, red_b, black_a, black_b):
                for half, to in spots:
                    buf[0, c, to, :] = value[8 * half : 8 * half + 8]
                    buf[pairs + 1, c, to, :] = zero

        def placed_rows(b, _):
            at = pl.ds(pl.multiple_of(16 * b, 16), 16)
            spots = [(half, pl.ds(pl.multiple_of(16 * b + EDGE + 8 * half, 8), 8)) for half in (0, 1)]
            for c in range(tiles + 1):
                fill(f32(placed[c, at, :]), c, spots)
            return 0

        lax.fori_loop(0, blocks, placed_rows, 0)
        for c in range(tiles + 1):
            fill(f32(small_prev[4 + c]), c, [(1, pl.ds(0, 8))])
            fill(f32(small_next[4 + c]), c, [(0, pl.ds(EDGE + rows, 8))])

        left_slot = (lane & 7) < 4

        def decode(q, left, right):
            left0, left1, right0, right1 = f32(left[0]), f32(left[1]), f32(right[0]), f32(right[1])
            items = (
                (left0[:8] + left0[8:], right0[:8] + right0[8:], 1.0),
                (left1[:8], right1[:8], 1.0 / 48.0),
                (left1[8:], right1[8:], 0.25),
            )
            for item, (a, b, scale) in enumerate(items):
                side[0, item, q] = jnp.where(left_slot, a, b) * scale
                side[1, item, q] = jnp.where(left_slot, b, a) * scale

        for q in range(blocks):
            decode(q, from_left[q], from_right[q])
        decode(blocks, small_prev[0:2], small_prev[2:4])
        decode(blocks + 1, small_next[0:2], small_next[2:4])

    @pl.when(g < pairs)
    def load():
        m = g
        slot = lax.rem(m, DEPTH)
        fields = ((red_a, sig_r, cur_r), (black_a, sig_b, cur_b))
        for colour in (0, 1):
            u_dst, s_dst, j_dst = fields[colour]
            for c in range(tiles):
                cols = slice(c * LANES, (c + 1) * LANES)
                both = f32(from_prev[colour, 0, :, cols])
                u_dst[m + 1, c, pl.ds(EDGE - 5, 8), :] = both[:8] + both[8:]
                s_dst[m, c, pl.ds(0, 8), :] = both[:8] * (1.0 / 48.0)
                j_dst[m, c, pl.ds(0, 8), :] = both[8:] * 0.25
                both = f32(from_next[colour, 0, :, cols])
                u_dst[m + 1, c, pl.ds(EDGE + rows, 8), :] = both[:8] + both[8:]
                s_dst[m, c, pl.ds(EDGE + rows - 5, 8), :] = both[:8] * (1.0 / 48.0)
                j_dst[m, c, pl.ds(EDGE + rows - 5, 8), :] = both[8:] * 0.25

        for copy in fetch(m):
            copy.wait()

        def own_rows(q, _):
            at = pl.ds(pl.multiple_of(16 * q, 16), 16)
            to = pl.ds(pl.multiple_of(16 * q + EDGE, 8), 16)
            for c in range(tiles):
                cols = slice(c * LANES, (c + 1) * LANES)
                a, b = u_buf[slot, 0, at, cols], u_buf[slot, 1, at, cols]
                red_a[m + 1, c, to, :] = jnp.where(even16, a, b)
                black_a[m + 1, c, to, :] = jnp.where(even16, b, a)
                a, b = f32(s_buf[slot, 0, at, cols]) * (1.0 / 48.0), f32(s_buf[slot, 1, at, cols]) * (1.0 / 48.0)
                sig_r[m, c, to, :] = jnp.where(even16, a, b)
                sig_b[m, c, to, :] = jnp.where(even16, b, a)
                a, b = f32(j_buf[slot, 0, at, cols]) * 0.25, f32(j_buf[slot, 1, at, cols]) * 0.25
                cur_r[m, c, to, :] = jnp.where(even16, a, b)
                cur_b[m, c, to, :] = jnp.where(even16, b, a)
            return 0

        lax.fori_loop(0, blocks, own_rows, 0)

        @pl.when(m + DEPTH < pairs)
        def fetch_more():
            for copy in fetch(m + DEPTH):
                copy.start()

        for colour in (0, 1):
            u_dst, s_dst, j_dst = fields[colour]
            for item, (dst, plane) in enumerate(((u_dst, m + 1), (s_dst, m), (j_dst, m))):
                for w in (0, 1):
                    turn = lax.rem(2 * LANES + 124 - 4 * colour - 8 * (m + pairs * w), LANES)
                    for q in range(blocks):
                        dst[plane, tiles, pl.ds(EDGE + 16 * q + 8 * w, 8), :] = pltpu.roll(side[colour, item, q], turn, 1)
                    if w == 1:
                        dst[plane, tiles, pl.ds(0, 8), :] = pltpu.roll(side[colour, item, blocks], turn, 1)
                    else:
                        dst[plane, tiles, pl.ds(EDGE + rows, 8), :] = pltpu.roll(side[colour, item, blocks + 1], turn, 1)

    def half_step(m, colour, own, other, sig, cur, start, count, outputs, write):
        def row_tile(at):
            centre = [other[m + 1, c, pl.ds(at, 8), :] for c in range(tiles + 1)]
            ahead = [pltpu.roll(x, 1, 1) for x in centre]
            back = [pltpu.roll(x, LANES - 1, 1) for x in centre]
            for c in range(outputs):
                left = jnp.where(lane_first, ahead[c - 1], ahead[c])
                right = jnp.where(lane_last, back[(c + 1) % (tiles + 1)], back[c])
                below = other[m, c, pl.ds(at, 8), :]
                above = other[m + 2, c, pl.ds(at, 8), :]
                outer = jnp.where(even8, below, above) if colour == 0 else jnp.where(even8, above, below)
                near = other[m + 1, c, pl.ds(at + 1, 8), :] - other[m + 1, c, pl.ds(at - 1, 8), :]
                far = own[m + 1, c, pl.ds(at + 2, 8), :] - own[m + 1, c, pl.ds(at - 2, 8), :]
                total = (left + right) + (centre[c] + outer)
                new = cur[m, c, pl.ds(at, 8), :] + 0.25 * total - sig[m, c, pl.ds(at, 8), :] * (8.0 * near - far)
                write(m, c, at, new)

        for r in range(count):
            row_tile(start + 8 * r)

    def keep(buf):
        def write(m, c, at, new):
            buf[m + 1, c, pl.ds(at, 8), :] = new

        return write

    def emit(m, c, at, new):
        red = red_a[m + 1, c, pl.ds(at, 8), :]
        cols = slice(c * LANES, (c + 1) * LANES)
        to = pl.ds(pl.multiple_of(at - EDGE, 8), 8)
        out_ref[0, to, cols] = jnp.where(even8, red, new)
        out_ref[1, to, cols] = jnp.where(even8, new, red)

    wide = (EDGE - 4, rows // 8 + 1, tiles + 1)
    last = (EDGE, rows // 8, tiles)
    plan = (
        (1, 0, red_a, black_a, sig_r, cur_r, wide, keep(red_b)),
        (2, 1, black_a, red_b, sig_b, cur_b, wide, keep(black_b)),
        (3, 0, red_b, black_b, sig_r, cur_r, wide, keep(red_a)),
        (4, 1, black_b, red_a, sig_b, cur_b, last, emit),
    )
    for lag, colour, own, other, sig, cur, where, write in plan:

        @pl.when((g >= lag) & (g < pairs + lag))
        def phase(lag=lag, colour=colour, own=own, other=other, sig=sig, cur=cur, where=where, write=write):
            half_step(g - lag, colour, own, other, sig, cur, *where, write)


def relax(placed, small_prev, small_next, from_left, from_right, from_prev, from_next, field, sigma, current):
    layers, rows, cols = field.shape
    pairs, tiles = layers // 2, cols // LANES
    ext = rows + 2 * EDGE

    def whole(array):
        zeros = (0,) * array.ndim
        return pl.BlockSpec(array.shape, lambda g: zeros)

    def coming(g):
        return jnp.minimum(g, pairs - 1)

    halo = pl.BlockSpec((2, 1, 16, cols), lambda g: (0, coming(g), 0, 0))
    block = pl.BlockSpec(memory_space=pl.ANY)
    fixed = [placed, small_prev, small_next]
    side = pl.BlockSpec((rows // 16, 2, 16, LANES), lambda g: (0, 0, 0, 0))
    state = pltpu.VMEM((pairs + 2, tiles + 1, ext, LANES), jnp.float32)
    coef = pltpu.VMEM((pairs, tiles + 1, ext, LANES), jnp.float32)
    return pl.pallas_call(
        functools.partial(relax_kernel, pairs=pairs, rows=rows, tiles=tiles),
        grid=(pairs + LAG,),
        in_specs=[whole(a) for a in fixed] + [side, side, halo, halo, block, block, block],
        out_specs=pl.BlockSpec((2, rows, cols), lambda g: (jnp.maximum(g - LAG, 0), 0, 0)),
        out_shape=jax.ShapeDtypeStruct(field.shape, jnp.float32),
        scratch_shapes=[state] * 4 + [coef] * 4 + [
            pltpu.VMEM((2, 3, rows // 16 + 2, 8, LANES), jnp.float32),
            pltpu.VMEM((DEPTH, 2, rows, cols), jnp.float32),
            pltpu.VMEM((DEPTH, 2, rows, cols), jnp.bfloat16),
            pltpu.VMEM((DEPTH, 2, rows, cols), jnp.bfloat16),
            pltpu.SemaphoreType.DMA((DEPTH, 3, 2)),
        ],
        compiler_params=pltpu.CompilerParams(vmem_limit_bytes=VMEM_BYTES),
        name="relax",
    )(*fixed, from_left, from_right, from_prev, from_next, field, sigma, current)


def moved(value, axis, steps):
    count = lax.axis_size(axis)
    return lax.ppermute(value, axis, [(i, (i + steps) % count) for i in range(count)])


def local(field, sigma, current, rotor_cycle, skew_list):
    rotor = [rotor_cycle] + [moved(rotor_cycle, "az", s) for s in range(2, lax.axis_size("az") - 1)]
    to_left, to_right = pack_cols(field, sigma, current, rotor_cycle)
    from_left, from_right = moved(to_right, "az", 1), moved(to_left, "az", -1)
    to_prev, to_next = pack_rows(field, sigma, current, to_left)
    from_prev, from_next = moved(to_next, "ta", 1), moved(to_prev, "ta", -1)
    small_to_prev, small_to_next = place_edges(rotor, skew_list, from_left, from_right)
    small_prev, small_next = moved(small_to_next, "ta", 1), moved(small_to_prev, "ta", -1)
    placed = place_cycle(rotor, skew_list, from_left, from_right, small_to_prev)
    return relax(
        placed, small_prev, small_next, from_left, from_right, from_prev, from_next, field, sigma, current
    )


def solution(mesh):
    placed = (P(None, "ta", "az"), P(None, "ta", "az"), P(None, "ta", "az"), P("ta", "az"), P("ta"))
    return jax.shard_map(
        local, mesh=mesh, in_specs=placed, out_specs=P(None, "ta", "az"), check_vma=False
    )
```

```python
import functools

import jax
import jax.numpy as jnp
from jax import lax
from jax.experimental import pallas as pl
from jax.experimental.pallas import tpu as pltpu
from jax.sharding import PartitionSpec as P

LANES = 128
EDGE = 8
LAG = 4
VMEM_BYTES = 60 * 1024 * 1024


def checker(rows):
    sub = lax.broadcasted_iota(jnp.int32, (rows, LANES), 0)
    lane = lax.broadcasted_iota(jnp.int32, (rows, LANES), 1)
    return ((sub + lane) & 1) == 0


def f32(value):
    return value.astype(jnp.float32)


def split_high_low(value):
    high = f32(value.astype(jnp.bfloat16))
    return high, value - high


def rows_kernel(u_top, u_bot, s_top, s_bot, j_top, j_bot, after, to_prev, to_next, *, pairs, tiles):
    even8 = checker(8)
    sub = lax.broadcasted_iota(jnp.int32, (8, LANES), 0)
    field_rows = sub < 5

    def pair_rows(m, _):
        for c in range(tiles):
            cols = slice(c * LANES, (c + 1) * LANES)
            for u_ref, s_ref, j_ref, half, out_ref in (
                (u_top, s_top, j_top, 0, to_prev),
                (u_bot, s_bot, j_bot, 8, to_next),
            ):
                eo = []
                for ref in (u_ref, s_ref, j_ref):
                    first = f32(ref[2 * m, :, cols])
                    second = f32(ref[2 * m + 1, :, cols])
                    if first.shape[0] == 16:
                        first = first[half : half + 8]
                        second = second[half : half + 8]
                    eo.append((first, second))
                for colour in (0, 1):
                    pick = [
                        jnp.where(even8, a, b) if colour == 0 else jnp.where(even8, b, a)
                        for a, b in eo
                    ]
                    high, low = split_high_low(pick[0])
                    sig, cur = pick[1], pick[2]
                    if half == 0:
                        sig = pltpu.roll(sig, 5, 0)
                        cur = pltpu.roll(cur, 5, 0)
                    else:
                        high = pltpu.roll(high, 5, 0)
                        low = pltpu.roll(low, 5, 0)
                    both = jnp.concatenate(
                        [jnp.where(field_rows, high, sig), jnp.where(field_rows, low, cur)], 0
                    )
                    out_ref[colour, m, :, cols] = both.astype(jnp.bfloat16)
        return 0

    lax.fori_loop(0, pairs, pair_rows, 0)


def cols_kernel(
    u_left, u_right, s_left, s_right, j_left, j_right, rotor, to_left, to_right, *, pairs, tiles, blocks
):
    even16 = checker(16)
    slot = lax.broadcasted_iota(jnp.int32, (8, LANES), 1) // 4
    slots = LANES // 4
    for q in range(blocks):
        rows = slice(16 * q, 16 * q + 16)
        for c in range(tiles):
            panel = rotor[rows, c * LANES : (c + 1) * LANES]
            to_left[q, 2 + c] = panel
            to_right[q, 2 + c] = panel
        for refs, out_ref, near_at, far_at in (
            ((u_left, s_left, j_left), to_left, 1, 2),
            ((u_right, s_right, j_right), to_right, 0, 1),
        ):
            packed = []
            for ref in refs:
                total = jnp.zeros((8, LANES), jnp.float32)
                for m in range(pairs):
                    first = f32(ref[2 * m, rows, :])
                    second = f32(ref[2 * m + 1, rows, :])
                    red = jnp.where(even16, first, second)
                    black = jnp.where(even16, second, first)
                    for w in (0, 1):
                        g = m + pairs * w
                        near = pltpu.roll(red[8 * w : 8 * w + 8], (8 * g + 4) % LANES, 1)
                        far = pltpu.roll(black[8 * w : 8 * w + 8], (8 * g + 8) % LANES, 1)
                        total = jnp.where(slot == (2 * g + near_at) % slots, near, total)
                        total = jnp.where(slot == (2 * g + far_at) % slots, far, total)
                packed.append(total)
            high, low = split_high_low(packed[0])
            out_ref[q, 0] = jnp.concatenate([high, low], 0).astype(jnp.bfloat16)
            out_ref[q, 1] = jnp.concatenate([packed[1], packed[2]], 0).astype(jnp.bfloat16)


def whole_at(shape, index):
    return pl.BlockSpec(shape, lambda i: index)


def pack_rows(field, sigma, current, after):
    layers, rows, cols = field.shape
    pairs, tiles = layers // 2, cols // LANES

    def row_specs(height):
        shape = (layers, height, cols)
        return [whole_at(shape, (0, 0, 0)), whole_at(shape, (0, rows // height - 1, 0))]

    shape = (2, pairs, 16, cols)
    return pl.pallas_call(
        functools.partial(rows_kernel, pairs=pairs, tiles=tiles),
        grid=(1,),
        in_specs=row_specs(8) + row_specs(16) * 2 + [pl.BlockSpec(memory_space=pl.ANY)],
        out_specs=[whole_at(shape, (0,) * 4)] * 2,
        out_shape=[jax.ShapeDtypeStruct(shape, jnp.bfloat16)] * 2,
        compiler_params=pltpu.CompilerParams(vmem_limit_bytes=VMEM_BYTES),
        cost_estimate=pl.CostEstimate(flops=0, bytes_accessed=12 << 20, transcendentals=0),
        name="pack_rows",
    )(field, field, sigma, sigma, current, current, after)


def pack_cols(field, sigma, current, rotor_cycle):
    layers, rows, cols = field.shape
    pairs, tiles, blocks = layers // 2, cols // LANES, rows // 16
    part = 2
    shape = (layers, 16 * part, LANES)
    col_specs = [pl.BlockSpec(shape, lambda i: (0, i, 0)), pl.BlockSpec(shape, lambda i: (0, i, tiles - 1))]
    out_spec = pl.BlockSpec((part, tiles + 2, 16, LANES), lambda i: (i, 0, 0, 0))
    return pl.pallas_call(
        functools.partial(cols_kernel, pairs=pairs, tiles=tiles, blocks=part),
        grid=(blocks // part,),
        in_specs=col_specs * 3 + [pl.BlockSpec((16 * part, cols), lambda i: (i, 0))],
        out_specs=[out_spec] * 2,
        out_shape=[jax.ShapeDtypeStruct((blocks, tiles + 2, 16, LANES), jnp.bfloat16)] * 2,
        compiler_params=pltpu.CompilerParams(vmem_limit_bytes=VMEM_BYTES),
        cost_estimate=pl.CostEstimate(flops=0, bytes_accessed=16 << 20, transcendentals=0),
        name="pack_cols",
    )(field, field, sigma, sigma, current, current, rotor_cycle)


def place_block(row, skew, rotor, from_left, from_right, at, slots, tiles):
    lane16 = lax.broadcasted_iota(jnp.int32, (16, LANES), 1)
    sub16 = lax.broadcasted_iota(jnp.int32, (16, LANES), 0)
    panels = slots * tiles
    bits = (panels - 1).bit_length()
    want = [(panels - tiles - 1 + p) % panels for p in range(tiles + 2)]
    needs = [set(want)]
    for bit in range(bits):
        needs.append(needs[-1] | {(q - (1 << bit)) % panels for q in needs[-1]})
    turn = jnp.zeros((16, LANES), jnp.int32)
    for i in range(16):
        turn = jnp.where(sub16 == i, skew[row + i], turn)

    def panel(steps, c):
        if steps in (1, slots - 1):
            return (from_left if steps == 1 else from_right)[at, 2 + c]
        source = rotor[0] if steps == 0 else rotor[steps - 1]
        return source[pl.ds(pl.multiple_of(16 * at, 16), 16), c * LANES : (c + 1) * LANES]

    cur = {q: f32(panel(slots - 1 - q // tiles, q % tiles)) for q in sorted(needs[bits])}
    for bit in reversed(range(bits)):
        on = ((turn >> bit) & 1) == 1
        cur = {q: jnp.where(on, cur[(q - (1 << bit)) % panels], cur[q]) for q in sorted(needs[bit])}
    placed = [cur[want[p + 1]] for p in range(tiles)]
    placed.append(jnp.where(lane16 < LANES // 2, cur[want[tiles + 1]], cur[want[0]]))
    return [x.astype(jnp.bfloat16) for x in placed]


def place_edges_kernel(skew, *refs, slots, rows, tiles):
    near, far, outs = refs[:slots], refs[slots : 2 * slots], refs[2 * slots :]
    for out_ref, ins, row in ((outs[0], near, 0), (outs[1], far, rows - 16)):
        from_left, from_right = ins[slots - 2 :]
        for i in (0, 1):
            out_ref[i] = from_left[0, i]
            out_ref[2 + i] = from_right[0, i]
        for c, value in enumerate(place_block(row, skew, ins[: slots - 2], from_left, from_right, 0, slots, tiles)):
            out_ref[4 + c] = value


def place_edges(rotor, skew_list, from_left, from_right):
    rows, cols = rotor[0].shape
    tiles, slots, blocks = cols // LANES, len(rotor) + 2, rows // 16

    def specs(i):
        side = whole_at((1, tiles + 2, 16, LANES), (i, 0, 0, 0))
        return [whole_at((16, cols), (i, 0))] * len(rotor) + [side, side]

    out = (tiles + 5, 16, LANES)
    ins = [*rotor, from_left, from_right]
    return pl.pallas_call(
        functools.partial(place_edges_kernel, slots=slots, rows=rows, tiles=tiles),
        grid=(1,),
        in_specs=[pl.BlockSpec(memory_space=pltpu.SMEM)] + specs(0) + specs(blocks - 1),
        out_specs=[whole_at(out, (0,) * 3)] * 2,
        out_shape=[jax.ShapeDtypeStruct(out, jnp.bfloat16)] * 2,
        compiler_params=pltpu.CompilerParams(vmem_limit_bytes=VMEM_BYTES),
        cost_estimate=pl.CostEstimate(flops=0, bytes_accessed=1 << 20, transcendentals=0),
        name="place_edges",
    )(skew_list, *ins, *ins)


def place_kernel(skew, *refs, slots, rows, tiles):
    rotor = refs[: slots - 2]
    from_left, from_right, after, placed_ref = refs[slots - 2 :]

    def rotor_rows(b, _):
        at = pl.ds(pl.multiple_of(16 * b, 16), 16)
        for p, value in enumerate(place_block(16 * b, skew, rotor, from_left, from_right, b, slots, tiles)):
            placed_ref[p, at, :] = value
        return 0

    lax.fori_loop(0, rows // 16, rotor_rows, 0)


def place_cycle(rotor, skew_list, from_left, from_right, after):
    rows, cols = rotor[0].shape
    tiles = cols // LANES
    sides = whole_at(from_left.shape, (0, 0, 0, 0))
    out = (tiles + 1, rows, LANES)
    return pl.pallas_call(
        functools.partial(place_kernel, slots=len(rotor) + 2, rows=rows, tiles=tiles),
        grid=(1,),
        in_specs=[pl.BlockSpec(memory_space=pltpu.SMEM)]
        + [whole_at((rows, cols), (0, 0))] * len(rotor)
        + [sides, sides, pl.BlockSpec(memory_space=pl.ANY)],
        out_specs=whole_at(out, (0,) * 3),
        out_shape=jax.ShapeDtypeStruct(out, jnp.bfloat16),
        compiler_params=pltpu.CompilerParams(vmem_limit_bytes=VMEM_BYTES),
        cost_estimate=pl.CostEstimate(flops=0, bytes_accessed=4 << 20, transcendentals=0),
        name="place_cycle",
    )(skew_list, *rotor, from_left, from_right, after)


def relax_kernel(placed, small_prev, small_next, from_left, from_right, from_prev, from_next,
     u_ref, s_ref, j_ref, out_ref,
     red_a, red_b, black_a, black_b, sig_r, sig_b, cur_r, cur_b, side, *, pairs, rows, tiles):
    g = pl.program_id(0)
    blocks = rows // 16
    even8 = checker(8)
    even16 = checker(16)
    lane = lax.broadcasted_iota(jnp.int32, (8, LANES), 1)
    lane_first = lane == 0
    lane_last = lane == LANES - 1

    @pl.when(g == 0)
    def prologue():
        def fill(value, c, spots):
            zero = jnp.zeros((8, LANES), jnp.float32)
            for buf in (red_a, red_b, black_a, black_b):
                for half, to in spots:
                    buf[0, c, to, :] = value[8 * half : 8 * half + 8]
                    buf[pairs + 1, c, to, :] = zero

        def placed_rows(b, _):
            at = pl.ds(pl.multiple_of(16 * b, 16), 16)
            spots = [(half, pl.ds(pl.multiple_of(16 * b + EDGE + 8 * half, 8), 8)) for half in (0, 1)]
            for c in range(tiles + 1):
                fill(f32(placed[c, at, :]), c, spots)
            return 0

        lax.fori_loop(0, blocks, placed_rows, 0)
        for c in range(tiles + 1):
            fill(f32(small_prev[4 + c]), c, [(1, pl.ds(0, 8))])
            fill(f32(small_next[4 + c]), c, [(0, pl.ds(EDGE + rows, 8))])

        left_slot = (lane & 7) < 4

        def decode(q, left, right):
            left0, left1, right0, right1 = f32(left[0]), f32(left[1]), f32(right[0]), f32(right[1])
            items = (
                (left0[:8] + left0[8:], right0[:8] + right0[8:], 1.0),
                (left1[:8], right1[:8], 1.0 / 48.0),
                (left1[8:], right1[8:], 0.25),
            )
            for item, (a, b, scale) in enumerate(items):
                side[0, item, q] = jnp.where(left_slot, a, b) * scale
                side[1, item, q] = jnp.where(left_slot, b, a) * scale

        for q in range(blocks):
            decode(q, from_left[q], from_right[q])
        decode(blocks, small_prev[0:2], small_prev[2:4])
        decode(blocks + 1, small_next[0:2], small_next[2:4])

        fields = ((red_a, sig_r, cur_r), (black_a, sig_b, cur_b))
        for m in range(pairs):
            for colour in (0, 1):
                for item, dst in enumerate(fields[colour]):
                    plane = m + 1 if item == 0 else m
                    for w in (0, 1):
                        turn = (2 * LANES + 124 - 4 * colour - 8 * (m + pairs * w)) % LANES
                        for q in range(blocks):
                            dst[plane, tiles, pl.ds(EDGE + 16 * q + 8 * w, 8), :] = pltpu.roll(side[colour, item, q], turn, 1)
                        end, at = (blocks, 0) if w == 1 else (blocks + 1, EDGE + rows)
                        dst[plane, tiles, pl.ds(at, 8), :] = pltpu.roll(side[colour, item, end], turn, 1)

    @pl.when(g < pairs)
    def load():
        m = g
        fields = ((red_a, sig_r, cur_r), (black_a, sig_b, cur_b))
        for colour in (0, 1):
            u_dst, s_dst, j_dst = fields[colour]
            for c in range(tiles):
                cols = slice(c * LANES, (c + 1) * LANES)
                both = f32(from_prev[colour, 0, :, cols])
                u_dst[m + 1, c, pl.ds(EDGE - 5, 8), :] = both[:8] + both[8:]
                s_dst[m, c, pl.ds(0, 8), :] = both[:8] * (1.0 / 48.0)
                j_dst[m, c, pl.ds(0, 8), :] = both[8:] * 0.25
                both = f32(from_next[colour, 0, :, cols])
                u_dst[m + 1, c, pl.ds(EDGE + rows, 8), :] = both[:8] + both[8:]
                s_dst[m, c, pl.ds(EDGE + rows - 5, 8), :] = both[:8] * (1.0 / 48.0)
                j_dst[m, c, pl.ds(EDGE + rows - 5, 8), :] = both[8:] * 0.25

        def own_rows(q, _):
            at = pl.ds(pl.multiple_of(16 * q, 16), 16)
            to = pl.ds(pl.multiple_of(16 * q + EDGE, 8), 16)
            for c in range(tiles):
                cols = slice(c * LANES, (c + 1) * LANES)
                a, b = u_ref[0, at, cols], u_ref[1, at, cols]
                red_a[m + 1, c, to, :] = jnp.where(even16, a, b)
                black_a[m + 1, c, to, :] = jnp.where(even16, b, a)
                a, b = f32(s_ref[0, at, cols]) * (1.0 / 48.0), f32(s_ref[1, at, cols]) * (1.0 / 48.0)
                sig_r[m, c, to, :] = jnp.where(even16, a, b)
                sig_b[m, c, to, :] = jnp.where(even16, b, a)
                a, b = f32(j_ref[0, at, cols]) * 0.25, f32(j_ref[1, at, cols]) * 0.25
                cur_r[m, c, to, :] = jnp.where(even16, a, b)
                cur_b[m, c, to, :] = jnp.where(even16, b, a)
            return 0

        lax.fori_loop(0, blocks, own_rows, 0)

    def half_step(m, colour, own, other, sig, cur, start, count, outputs, write):
        def row_tile(at):
            centre = [other[m + 1, c, pl.ds(at, 8), :] for c in range(tiles + 1)]
            ahead = [pltpu.roll(x, 1, 1) for x in centre]
            back = [pltpu.roll(x, LANES - 1, 1) for x in centre]
            for c in range(outputs):
                left = jnp.where(lane_first, ahead[c - 1], ahead[c])
                right = jnp.where(lane_last, back[(c + 1) % (tiles + 1)], back[c])
                below = other[m, c, pl.ds(at, 8), :]
                above = other[m + 2, c, pl.ds(at, 8), :]
                outer = jnp.where(even8, below, above) if colour == 0 else jnp.where(even8, above, below)
                near = other[m + 1, c, pl.ds(at + 1, 8), :] - other[m + 1, c, pl.ds(at - 1, 8), :]
                far = own[m + 1, c, pl.ds(at + 2, 8), :] - own[m + 1, c, pl.ds(at - 2, 8), :]
                total = (left + right) + (centre[c] + outer)
                new = cur[m, c, pl.ds(at, 8), :] + 0.25 * total - sig[m, c, pl.ds(at, 8), :] * (8.0 * near - far)
                write(m, c, at, new)

        for r in range(count):
            row_tile(start + 8 * r)

    def keep(buf):
        def write(m, c, at, new):
            buf[m + 1, c, pl.ds(at, 8), :] = new

        return write

    def emit(m, c, at, new):
        red = red_a[m + 1, c, pl.ds(at, 8), :]
        cols = slice(c * LANES, (c + 1) * LANES)
        to = pl.ds(pl.multiple_of(at - EDGE, 8), 8)
        out_ref[0, to, cols] = jnp.where(even8, red, new)
        out_ref[1, to, cols] = jnp.where(even8, new, red)

    wide = (EDGE - 4, rows // 8 + 1, tiles + 1)
    last = (EDGE, rows // 8, tiles)
    plan = (
        (1, 0, red_a, black_a, sig_r, cur_r, wide, keep(red_b)),
        (2, 1, black_a, red_b, sig_b, cur_b, wide, keep(black_b)),
        (3, 0, red_b, black_b, sig_r, cur_r, wide, keep(red_a)),
        (4, 1, black_b, red_a, sig_b, cur_b, last, emit),
    )
    for lag, colour, own, other, sig, cur, where, write in plan:

        @pl.when((g >= lag) & (g < pairs + lag))
        def phase(lag=lag, colour=colour, own=own, other=other, sig=sig, cur=cur, where=where, write=write):
            half_step(g - lag, colour, own, other, sig, cur, *where, write)


def relax(placed, small_prev, small_next, from_left, from_right, from_prev, from_next, field, sigma, current):
    layers, rows, cols = field.shape
    pairs, tiles = layers // 2, cols // LANES
    ext = rows + 2 * EDGE

    def whole(array):
        zeros = (0,) * array.ndim
        return pl.BlockSpec(array.shape, lambda g: zeros)

    def coming(g):
        return jnp.minimum(g, pairs - 1)

    halo = pl.BlockSpec((2, 1, 16, cols), lambda g: (0, coming(g), 0, 0))
    block = pl.BlockSpec((2, rows, cols), lambda g: (coming(g), 0, 0))
    fixed = [placed, small_prev, small_next]
    side = pl.BlockSpec((rows // 16, 2, 16, LANES), lambda g: (0, 0, 0, 0))
    state = pltpu.VMEM((pairs + 2, tiles + 1, ext, LANES), jnp.float32)
    coef = pltpu.VMEM((pairs, tiles + 1, ext, LANES), jnp.float32)
    return pl.pallas_call(
        functools.partial(relax_kernel, pairs=pairs, rows=rows, tiles=tiles),
        grid=(pairs + LAG,),
        in_specs=[whole(a) for a in fixed] + [side, side, halo, halo, block, block, block],
        out_specs=pl.BlockSpec((2, rows, cols), lambda g: (jnp.maximum(g - LAG, 0), 0, 0)),
        out_shape=jax.ShapeDtypeStruct(field.shape, jnp.float32),
        scratch_shapes=[state] * 4 + [coef] * 4 + [pltpu.VMEM((2, 3, rows // 16 + 2, 8, LANES), jnp.float32)],
        compiler_params=pltpu.CompilerParams(vmem_limit_bytes=VMEM_BYTES),
        name="relax",
    )(*fixed, from_left, from_right, from_prev, from_next, field, sigma, current)


def moved(value, axis, steps):
    count = lax.axis_size(axis)
    return lax.ppermute(value, axis, [(i, (i + steps) % count) for i in range(count)])


def local(field, sigma, current, rotor_cycle, skew_list):
    rotor = [rotor_cycle] + [moved(rotor_cycle, "az", s) for s in range(2, lax.axis_size("az") - 1)]
    to_left, to_right = pack_cols(field, sigma, current, rotor_cycle)
    from_left, from_right = moved(to_right, "az", 1), moved(to_left, "az", -1)
    to_prev, to_next = pack_rows(field, sigma, current, to_left)
    from_prev, from_next = moved(to_next, "ta", 1), moved(to_prev, "ta", -1)
    small_to_prev, small_to_next = place_edges(rotor, skew_list, from_left, from_right)
    small_prev, small_next = moved(small_to_next, "ta", 1), moved(small_to_prev, "ta", -1)
    placed = place_cycle(rotor, skew_list, from_left, from_right, small_to_prev)
    return relax(
        placed, small_prev, small_next, from_left, from_right, from_prev, from_next, field, sigma, current
    )


def solution(mesh):
    placed = (P(None, "ta", "az"), P(None, "ta", "az"), P(None, "ta", "az"), P("ta", "az"), P("ta"))
    return jax.shard_map(
        local, mesh=mesh, in_specs=placed, out_specs=P(None, "ta", "az"), check_vma=False
    )
```
